32 devices in a mesh: gx: 4 (over z), gy: 4 (over x, core), ga: 2 (over y).
Axes of the slice: x: 2, y: 2, z: 4, core: 2. Of those that a mesh axis runs over, the one named last changes fastest.
Arguments:
- velocity: float32 [2, 80, 64, 512], P(None, None, ('gy', 'ga'), 'gx'), may hold values from -4 to 4
- tracers: float32 [2, 80, 64, 512], P(None, None, ('gy', 'ga'), 'gx'), may hold values from -6 to 6
- mixing: float32 [80, 64, 512], P(None, ('gy', 'ga'), 'gx'), may hold values from 0.05 to 400
- thickness: float32 [80], replicated, may hold values from 0.5 to 4
- coriolis: float32 [64], P(('gy', 'ga')), may hold values from -1.5 to 1.5
- land: int32 [64, 512], P(('gy', 'ga'), 'gx'), may hold values 0 or 1
- bottom: int32 [64, 512], P(('gy', 'ga'), 'gx'), may hold values from 70 to 80
- surface: float32 [64, 512], P(('gy', 'ga'), 'gx'), may hold values from -4 to 4
- barotropic: float32 [2, 64, 512], P(None, ('gy', 'ga'), 'gx'), may hold values from -3 to 3
Outputs:
- new_velocity: float32 [2, 80, 64, 512], P(None, None, ('gy', 'ga'), 'gx')
- new_tracers: float32 [2, 80, 64, 512], P(None, None, ('gy', 'ga'), 'gx')
- new_surface: float32 [64, 512], P(('gy', 'ga'), 'gx')
- new_barotropic: float32 [2, 64, 512], P(None, ('gy', 'ga'), 'gx')
The draws below stay inside these ranges and needn't reach their ends.
All inputs are finite; a program needn't handle non-finite values. No bound on the sum of `land` on one device may be relied on, other than what follows from the above.
Results may differ from the reference program's by a relative error of at most 0.0003.
Values sent between devices are 32-bit elements; how exact they have to be, the bound alone decides.
A program may use at most 64 MiB of HBM per device.

```python
import math
import jax
import jax.numpy as jnp
from jax import lax

NZ = 80
NSUB = 30
NX = 512
NY = 64
N_GX = 4


def draw_mixing(key, part):
    base_key, rough_key = jax.random.split(jax.random.fold_in(key, 11))
    lowest = 0.1
    base = jnp.exp(jax.random.uniform(base_key, (NY, NX), jnp.float32, math.log(lowest), math.log(200.0)))
    rough = jnp.exp(jax.random.uniform(rough_key, (NZ, NY, NX), jnp.float32, math.log(0.5), math.log(2.0)))
    return base[None] * rough


def draw_surface(key, part):
    noise_key = jax.random.fold_in(jax.random.fold_in(key, 23), 0)
    return 0.5 * jax.random.truncated_normal(noise_key, -8.0, 8.0, (NY, NX), jnp.float32)


def set_ends(entries, rng, smallest, largest):
    spot = [jax.random.randint(jax.random.fold_in(rng, axis), (), 0, length) for axis, length in enumerate(entries.shape)]
    widest = entries.shape.index(max(entries.shape))
    next_to = spot[:widest] + [(spot[widest] + 1) % entries.shape[widest]] + spot[widest + 1:]
    return entries.at[tuple(spot)].set(smallest).at[tuple(next_to)].set(largest)


def level_of(rng, shape, cuts, smallest, top_value):
    gain, own = 1.0, jax.random.fold_in(rng, 6)
    for axis_at, blocks in cuts:
        steps = jnp.exp(jax.random.uniform(jax.random.fold_in(own, axis_at), (blocks,), jnp.float32, smallest / len(cuts), top_value / len(cuts)))
        gain = gain * jnp.repeat(steps, shape[axis_at] // blocks).reshape([-1 if axis == axis_at else 1 for axis in range(len(shape))])
    return gain


def noise(rng, dims, spread, limit, shards=(), kind=jnp.bfloat16):
    array = jax.random.normal(rng, dims, jnp.float32) * spread
    if len(shards) > 0:
        array = level_of(rng, dims, shards, -0.22, 0.18) * array
    return jnp.clip(array, min=-limit, max=limit).astype(kind)


def setup_inputs(seed: int = 0) -> dict:
    splits = jax.random.split(jax.random.key(seed), 10)
    velocity = noise(splits[0], (2, NZ, NY, NX), 0.5, 4.0, ((2, 8), (3, 4)), jnp.float32)
    tracers = noise(splits[1], (2, NZ, NY, NX), 1.0, 6.0, ((2, 8), (3, 4)), jnp.float32)
    mixing = draw_mixing(jax.random.fold_in(splits[9], 71), 0)
    thickness = jnp.clip(jnp.exp(jax.random.uniform(splits[3], (NZ,), jnp.float32, math.log(0.5), math.log(4.0))), 0.5, 4.0)
    coriolis = jnp.clip(jax.random.uniform(splits[4], (NY,), jnp.float32, -1.5, 1.5) * level_of(splits[4], (NY,), ((0, 8),), -0.4, 0.0), -1.5, 1.5)
    land = set_ends((jax.random.randint(splits[5], (NY, NX), 0, 50) < 49).astype(jnp.int32), jax.random.fold_in(splits[5], 1), 0, 1)
    bottom = set_ends(jax.random.randint(splits[6], (NY, NX), NZ - NZ // 8, NZ + 1), jax.random.fold_in(splits[6], 1), NZ - NZ // 8, NZ).astype(jnp.int32)
    surface = draw_surface(jax.random.fold_in(splits[9], 71), 0)
    barotropic = noise(splits[8], (2, NY, NX), 0.3, 3.0, ((1, 8), (2, 4)), jnp.float32)
    return dict(velocity=velocity, tracers=tracers, mixing=mixing, thickness=thickness, coriolis=coriolis, land=land, bottom=bottom, surface=surface, barotropic=barotropic)


step_main = 0.1
visc_four = 0.02
diff_four = 0.02
press_scale = 0.02
step_baro = 0.1
grav_baro = 25.0
expand_temp = 0.2
contract_salt = 0.1


def laplace(quantity, wet_mask):
    centre = quantity[..., 1:-1, 1:-1]
    beside_all = quantity[..., 1:-1, 2:] + quantity[..., 1:-1, :-2] + quantity[..., 2:, 1:-1] + quantity[..., :-2, 1:-1]
    return (beside_all - 4.0 * centre) * wet_mask[..., 1:-1, 1:-1]


def diff_x(quantity):
    return 0.5 * (quantity[..., 2:-2, 3:-1] - quantity[..., 2:-2, 1:-3])


def diff_y(quantity):
    return 0.5 * (quantity[..., 3:-1, 2:-2] - quantity[..., 1:-3, 2:-2])


def tendency(padded, pressure, coriolis):
    east_vel = padded[0]
    north_vel = padded[1]
    wet_mask = padded[4]
    inner_wet = wet_mask[..., 2:-2, 2:-2]
    rotate = coriolis[:, None]
    changes = []
    for component in range(4):
        quantity = padded[component]
        advect = diff_x(east_vel * quantity) + diff_y(north_vel * quantity)
        smooth = laplace(laplace(quantity, wet_mask), wet_mask[..., 1:-1, 1:-1])
        if component == 0:
            change = rotate * north_vel[..., 2:-2, 2:-2] - diff_x(pressure) - visc_four * smooth
        elif component == 1:
            change = -rotate * east_vel[..., 2:-2, 2:-2] - diff_y(pressure) - visc_four * smooth
        else:
            change = -diff_four * smooth
        changes.append((change - advect) * inner_wet)
    return jnp.stack(changes)


def vertical_solve(provisional, mixing, wet_mask, thickness):
    levels = thickness.shape[0]
    tail_ones = (1,) * (mixing.ndim - 1)
    depth_col = thickness.reshape((levels,) + tail_ones)
    middle = (0.5 * (thickness[:-1] + thickness[1:])).reshape((levels - 1,) + tail_ones)
    coupling = mixing[:-1] * wet_mask[:-1] * wet_mask[1:] / middle
    zeros_row = jnp.zeros((1,) + mixing.shape[1:], jnp.float32)
    below_link = jnp.concatenate([coupling, zeros_row], axis=0)
    upper_link = jnp.concatenate([zeros_row, coupling], axis=0)
    diagonal = depth_col + upper_link + below_link
    source = depth_col[:, None] * provisional

    def forward(sweep, inputs):
        ratio_prev, value_prev = sweep
        upper_now, diag_now, below_now, source_now = inputs
        divisor = diag_now - upper_now * ratio_prev
        sweep_ratio = below_now / divisor
        sweep_value = (source_now + upper_now[None] * value_prev) / divisor[None]
        return (sweep_ratio, sweep_value), (sweep_ratio, sweep_value)

    start_sweep = (jnp.zeros(mixing.shape[1:], jnp.float32), jnp.zeros(provisional.shape[1:], jnp.float32))
    unused, (ratios, values) = lax.scan(forward, start_sweep, (upper_link, diagonal, below_link, source))

    def backward(following, inputs):
        sweep_ratio, sweep_value = inputs
        result = sweep_value + sweep_ratio[None] * following
        return result, result

    unused_last, solved = lax.scan(backward, jnp.zeros(provisional.shape[1:], jnp.float32), (ratios, values), reverse=True)
    return solved


def zero_diff(quantity, along):
    extent = quantity.shape[along]
    ahead_part = lax.slice_in_dim(quantity, 1, extent, axis=along)
    behind = lax.slice_in_dim(quantity, 0, extent - 1, axis=along)
    zeros_row = jnp.zeros_like(lax.slice_in_dim(quantity, 0, 1, axis=along))
    return 0.5 * (jnp.concatenate([ahead_part, zeros_row], axis=along) - jnp.concatenate([zeros_row, behind], axis=along))


def roll_east(quantity):
    return 0.5 * (jnp.roll(quantity, -1, axis=-1) - jnp.roll(quantity, 1, axis=-1))


def north_zero(quantity):
    return zero_diff(quantity, quantity.ndim - 2)


def baro_step(baro_state, statics, east_diff, north_diff):
    height = baro_state[0]
    east_vel = baro_state[1]
    north_vel = baro_state[2]
    depth_ratio = statics[0]
    sea_mask = statics[1]
    rotate = statics[2]
    push_east = statics[3]
    push_north = statics[4]
    new_height = (height - step_baro * (east_diff(depth_ratio * east_vel) + north_diff(depth_ratio * north_vel))) * sea_mask
    new_east = (east_vel + step_baro * (push_east + rotate * north_vel - grav_baro * east_diff(new_height))) * sea_mask
    new_north = (north_vel + step_baro * (push_north - rotate * east_vel - grav_baro * north_diff(new_height))) * sea_mask
    return jnp.stack([new_height, new_east, new_north])


def pad_field(quantity, halo_width):
    wrapped = jnp.concatenate([quantity[..., -halo_width:], quantity, quantity[..., :halo_width]], axis=-1)
    zeros_rows = jnp.zeros(wrapped.shape[:-2] + (halo_width, wrapped.shape[-1]), jnp.float32)
    return jnp.concatenate([zeros_rows, wrapped, zeros_rows], axis=-2)


def reference(velocity, tracers, mixing, thickness, coriolis, land, bottom, surface, barotropic):
    levels = thickness.shape[0]
    land_f = land.astype(jnp.float32)

    def level_step(loop_carry, level_index):
        overlying, forcing, depth_sum = loop_carry
        wet_level = land_f * (level_index < bottom).astype(jnp.float32)
        velocity_level = lax.dynamic_index_in_dim(velocity, level_index, 1, keepdims=False) * wet_level[None]
        tracer_level = lax.dynamic_index_in_dim(tracers, level_index, 1, keepdims=False) * wet_level[None]
        stacked = jnp.concatenate([velocity_level, tracer_level, wet_level[None]], axis=0)
        padded = pad_field(stacked, 2)
        layer_dz = thickness[level_index]
        weight = (contract_salt * padded[3] - expand_temp * padded[2]) * padded[4] * layer_dz
        pressure = press_scale * (overlying + 0.5 * weight)
        growth = tendency(padded, pressure, coriolis)
        provisional = stacked[:4] + step_main * growth
        return (overlying + weight, forcing + layer_dz * growth[:2], depth_sum + layer_dz * wet_level), provisional

    start_carry = (jnp.zeros((land.shape[0] + 4, land.shape[1] + 4), jnp.float32),
                   jnp.zeros((2,) + land.shape, jnp.float32), jnp.zeros(land.shape, jnp.float32))
    (unused, forcing, depth_sum), provisional = lax.scan(level_step, start_carry, jnp.arange(levels, dtype=jnp.int32))

    level_ids = jnp.arange(levels, dtype=jnp.int32).reshape((levels, 1, 1))
    wet_full = land_f[None] * (level_ids < bottom[None]).astype(jnp.float32)

    blocks = N_GX
    block_cols = land.shape[1] // blocks

    def block_solve(block_index):
        start = (block_index * block_cols).astype(jnp.int32)
        return vertical_solve(lax.dynamic_slice_in_dim(provisional, start, block_cols, 3),
                              lax.dynamic_slice_in_dim(mixing, start, block_cols, 2),
                              lax.dynamic_slice_in_dim(wet_full, start, block_cols, 2), thickness)

    pieces = lax.map(block_solve, jnp.arange(blocks, dtype=jnp.int32))
    solved = jnp.moveaxis(pieces, 0, -2).reshape(provisional.shape)

    safe_depth = jnp.maximum(depth_sum, 1.0)
    statics = jnp.stack([depth_sum / jnp.sum(thickness), land_f, coriolis[:, None] * jnp.ones_like(land_f),
                         forcing[0] / safe_depth * land_f, forcing[1] / safe_depth * land_f])
    start_state = jnp.concatenate([surface[None], barotropic], axis=0)

    def substep(turn_index, loop_carry):
        baro_state, total_sum = loop_carry
        baro_state = baro_step(baro_state, statics, roll_east, north_zero)
        return baro_state, total_sum + baro_state[1:]

    baro_state, total_sum = lax.fori_loop(0, NSUB, substep, (start_state, jnp.zeros((2,) + land.shape, jnp.float32)))
    average = total_sum / NSUB

    thick_col = thickness.reshape((levels, 1, 1, 1))
    depth_mean = jnp.sum(thick_col * wet_full[:, None] * solved[:, :2], axis=0) / safe_depth
    new_velocity = (jnp.moveaxis(solved[:, :2], 0, 1) - depth_mean[:, None] + average[:, None]) * wet_full[None]
    new_tracers = jnp.moveaxis(solved[:, 2:], 0, 1)
    return new_velocity, new_tracers, baro_state[0], baro_state[1:]
```

```python
import functools
import jax
import jax.numpy as jnp
from jax import lax
from jax.experimental import pallas as pl
from jax.experimental.pallas import tpu as pltpu
from jax.sharding import PartitionSpec as P

NSUB = 30
F32 = jnp.float32
MESH = pl.DeviceIdType.MESH
CHUNKS = 5


def kernel(
    nx, ngy, nga, levels,
    vel, trc, mix, dz, cor, land, bot, surf, baro,
    vel_out, trc_out, surf_out, baro_out,
    ynorth, ysouth, hnorth, hsouth,
    xpack, xrecv, crn, crs, bq, bl, bcorn,
    tile2, t2recv, wide1, all1, push1, p2recv, wide2, all2,
    ratio_buf, val_buf, send_sem, recv_sem,
):
    tiles = ngy * nga
    groups = xpack.shape[1]
    per_chunk = levels // CHUNKS
    gx = lax.axis_index("gx")
    t = lax.axis_index("gy") * nga + lax.axis_index("ga")
    left = lax.rem(gx + nx - 1, nx)
    right = lax.rem(gx + 1, nx)
    has_n = t < tiles - 1
    has_s = t > 0

    def dev(x, tile):
        return {"gx": x, "gy": tile // nga, "ga": lax.rem(tile, nga)}

    up = jnp.minimum(t + 1, tiles - 1)
    down = jnp.maximum(t - 1, 0)

    barrier = pltpu.get_barrier_semaphore()

    def greet(d):
        pl.semaphore_signal(barrier, inc=1, device_id=d, device_id_type=MESH)

    greet(dev(left, t))
    greet(dev(right, t))
    for p in range(1, tiles):
        greet(dev(gx, lax.rem(t + p, tiles)))

    @pl.when(has_n)
    def _():
        greet(dev(left, up))
        greet(dev(right, up))

    @pl.when(has_s)
    def _():
        greet(dev(left, down))
        greet(dev(right, down))

    row = lax.broadcasted_iota(jnp.int32, (8, 128), 0)
    lane = lax.broadcasted_iota(jnp.int32, (8, 128), 1)
    slot = lane // 4
    l4 = lane - 4 * slot
    first_l, last_l = lane == 0, lane == 127
    first_r, last_r = row == 0, row == 7

    land_i = land[...]
    be = jnp.where(land_i > 0, bot[...], -1).astype(F32)
    land_f = land_i.astype(F32)

    def depth_body(k, acc):
        total, depth = acc
        d = dz[k]
        wet = jnp.where(k.astype(F32) < be, 1.0, 0.0)
        return total + d, depth + d * wet

    dz_total, depth_sum = lax.fori_loop(
        0, levels, depth_body, (jnp.float32(0.0), jnp.zeros((8, 128), F32))
    )
    safe = jnp.maximum(depth_sum, 1.0)
    rot = jnp.zeros((8, 128), F32)
    for r in range(8):
        rot = jnp.where(row == r, cor[r], rot)
    tile2[0] = surf[...]
    tile2[1] = baro[0]
    tile2[2] = baro[1]
    tile2[3] = be
    tile2[4] = depth_sum / jnp.broadcast_to(dz_total, (8, 128))
    tile2[5] = rot

    pl.semaphore_wait(
        barrier, 2 + tiles - 1 + jnp.where(has_n, 2, 0) + jnp.where(has_s, 2, 0)
    )

    def rc(src, dst, i, d):
        return pltpu.make_async_remote_copy(
            src_ref=src, dst_ref=dst, send_sem=send_sem.at[i], recv_sem=recv_sem.at[i],
            device_id=d, device_id_type=MESH,
        )

    index = [0]

    def nxt():
        index[0] += 1
        return index[0] - 1

    def rows_of(tile):
        return pl.ds(pl.multiple_of(tile * 8, 8), 8)

    def pair(src, recv):
        return [
            rc(src, recv.at[0], nxt(), dev(right, t)),
            rc(src, recv.at[1], nxt(), dev(left, t)),
        ]

    def peers(src, dst):
        starts, waits = [], []
        for p in range(1, tiles):
            i = nxt()
            to = lax.rem(t + p, tiles)
            origin = lax.rem(t + tiles - p, tiles)
            starts.append(rc(src, dst.at[:, rows_of(t), :], i, dev(gx, to)))
            waits.append(rc(src, dst.at[:, rows_of(origin), :], i, dev(gx, to)))
        return starts, waits

    two_d = pair(tile2, t2recv)
    for c in two_d:
        c.start()

    @pl.when(jnp.logical_not(has_n))
    def _():
        hnorth[...] = jnp.zeros_like(hnorth)
        crn[...] = jnp.zeros_like(crn)

    @pl.when(jnp.logical_not(has_s))
    def _():
        hsouth[...] = jnp.zeros_like(hsouth)
        crs[...] = jnp.zeros_like(crs)

    xpack[...] = jnp.zeros_like(xpack)

    def field(c, k):
        return vel[c, k] if c < 2 else trc[c - 2, k]

    def pack_body(k, carry):
        wet = k.astype(F32) < be
        g = k // 32
        m = k - 32 * g
        q = [jnp.where(wet, field(c, k), 0.0) for c in range(4)]
        yn = jnp.concatenate([a[6:8] for a in q], axis=0)
        ys = jnp.concatenate([a[0:2] for a in q], axis=0)
        ynorth[k] = yn
        ysouth[k] = ys
        here = slot == m
        for c, a in enumerate(q + [yn, ys]):
            xpack[c, g] = jnp.where(here, pltpu.roll(a, 2 + 4 * m, 1), xpack[c, g])
        return carry

    to_north, to_south = [], []
    for n in range(CHUNKS):
        span = pl.ds(n * per_chunk, per_chunk)
        lax.fori_loop(n * per_chunk, (n + 1) * per_chunk, pack_body, 0)
        to_north.append(rc(ynorth.at[span], hsouth.at[span], nxt(), dev(gx, up)))
        to_south.append(rc(ysouth.at[span], hnorth.at[span], nxt(), dev(gx, down)))
        pl.when(has_n)(to_north[-1].start)
        pl.when(has_s)(to_south[-1].start)

    x_copies = pair(xpack.at[pl.ds(0, 4)], xrecv)
    for c in x_copies:
        c.start()
    diag_n = [
        rc(xpack.at[4], crs.at[1], nxt(), dev(left, up)),
        rc(xpack.at[4], crs.at[0], nxt(), dev(right, up)),
    ]
    diag_s = [
        rc(xpack.at[5], crn.at[1], nxt(), dev(left, down)),
        rc(xpack.at[5], crn.at[0], nxt(), dev(right, down)),
    ]
    for c in diag_n:
        pl.when(has_n)(c.start)
    for c in diag_s:
        pl.when(has_s)(c.start)

    for c in two_d:
        c.wait_recv()
    for f in range(6):
        wide1[f, :, 0:128] = tile2[f]
        wide1[f, :, 128:256] = jnp.where(lane < 64, t2recv[1, f], t2recv[0, f])
    starts1, waits1 = peers(wide1, all1)
    for c in starts1:
        c.start()
    all1[:, rows_of(t), :] = wide1[...]

    be_side = jnp.where(
        l4 == 1,
        jnp.broadcast_to(t2recv[0, 3][:, 127:128], (8, 128)),
        jnp.broadcast_to(t2recv[1, 3][:, 0:1], (8, 128)),
    )
    for c in x_copies:
        c.wait_recv()
    for c in diag_n:
        pl.when(has_s)(c.wait_recv)
    for c in diag_s:
        pl.when(has_n)(c.wait_recv)

    def close(a):
        return jnp.where(l4 == 1, a, pltpu.roll(a, 126, 1))

    low = l4 < 2
    for g in range(groups):
        corner_n = jnp.where(low, crn[0, g], crn[1, g])
        corner_s = jnp.where(low, crs[0, g], crs[1, g])
        bcorn[0, g] = close(corner_n)
        bcorn[1, g] = close(corner_s)
        wet = (32 * g + slot).astype(F32) < be_side
        for c in range(4):
            a = jnp.where(low, xrecv[0, c, g], xrecv[1, c, g])
            mine = xpack[c, g]
            sides = jnp.where(
                l4 == 1,
                pltpu.roll(a, 1, 1) + pltpu.roll(mine, 127, 1),
                pltpu.roll(a, 127, 1) + pltpu.roll(mine, 1, 1),
            )
            north = jnp.where(
                last_r, jnp.broadcast_to(corner_n[2 * c:2 * c + 1], (8, 128)), pltpu.roll(a, 7, 0)
            )
            south = jnp.where(
                first_r, jnp.broadcast_to(corner_s[2 * c + 1:2 * c + 2], (8, 128)), pltpu.roll(a, 1, 0)
            )
            lap = jnp.where(wet, sides + north + south - 4.0 * a, 0.0)
            bq[c, g] = close(a)
            bl[c, g] = close(lap)

    for c in waits1:
        c.wait_recv()
    be_n = jnp.where(
        has_n, jnp.broadcast_to(all1[3, rows_of(up), 0:128][0:1], (8, 128)), -1.0
    )
    be_s = jnp.where(
        has_s, jnp.broadcast_to(all1[3, rows_of(down), 0:128][7:8], (8, 128)), -1.0
    )

    def east_west(a, h):
        return (
            jnp.where(last_l, h, pltpu.roll(a, 127, 1)),
            jnp.where(first_l, h, pltpu.roll(a, 1, 1)),
        )

    def row_of(a, r):
        return jnp.broadcast_to(a[r:r + 1], (8, 128))

    def level_body(k, carry):
        acc_x, acc_y, force_u, force_v, e_up, ratio, values = carry
        kf = k.astype(F32)
        d = dz[k]
        k_next = jnp.minimum(k + 1, levels - 1)
        d_next = dz[k_next]
        g = k // 32
        turn = 127 - 4 * (k - 32 * g)
        wet = kf < be
        wet_next = jnp.logical_and(kf + 1.0 < be, k + 1 < levels)
        q = [jnp.where(wet, field(c, k), 0.0) for c in range(4)]
        hn, hs = hnorth[k], hsouth[k]
        he, hw = east_west(hn, pltpu.roll(bcorn[0, g], turn, 1))
        lap_n = jnp.where(
            kf < be_n, pltpu.roll(hn + ynorth[k], 7, 0) + he + hw - 4.0 * hn, 0.0
        )
        he, hw = east_west(hs, pltpu.roll(bcorn[1, g], turn, 1))
        lap_s = jnp.where(
            kf < be_s, pltpu.roll(hs + ysouth[k], 1, 0) + he + hw - 4.0 * hs, 0.0
        )
        around, smooth = [], []
        for c in range(4):
            a = q[c]
            e, w = east_west(a, pltpu.roll(bq[c, g], turn, 1))
            n = jnp.where(last_r, row_of(hn, 2 * c), pltpu.roll(a, 7, 0))
            s = jnp.where(first_r, row_of(hs, 2 * c + 1), pltpu.roll(a, 1, 0))
            around.append((e, w, n, s))
            lap = jnp.where(wet, (e + w) + (n + s) - 4.0 * a, 0.0)
            e, w = east_west(lap, pltpu.roll(bl[c, g], turn, 1))
            n = jnp.where(last_r, row_of(lap_n, 2 * c), pltpu.roll(lap, 7, 0))
            s = jnp.where(first_r, row_of(lap_s, 2 * c + 1), pltpu.roll(lap, 1, 0))
            smooth.append(0.02 * ((e + w) + (n + s) - 4.0 * lap))
        weights = [
            (0.1 * around[3][i] - 0.2 * around[2][i]) * d for i in range(4)
        ]
        slope_x = weights[0] - weights[1]
        slope_y = weights[2] - weights[3]
        press_x = 0.01 * (acc_x + 0.5 * slope_x)
        press_y = 0.01 * (acc_y + 0.5 * slope_y)
        acc_x = acc_x + slope_x
        acc_y = acc_y + slope_y
        ue, uw = around[0][0], around[0][1]
        vn, vs = around[1][2], around[1][3]
        extra = [rot * q[1] - press_x, -rot * q[0] - press_y, 0.0, 0.0]
        growth = []
        for c in range(4):
            e, w, n, s = around[c]
            advect = 0.5 * ((ue * e - uw * w) + (vn * n - vs * s))
            growth.append(jnp.where(wet, extra[c] - smooth[c] - advect, 0.0))
        force_u = force_u + d * growth[0]
        force_v = force_v + d * growth[1]
        e_now = jnp.where(
            jnp.logical_and(wet, wet_next), mix[k] / (0.5 * (d + d_next)), 0.0
        )
        inverse = 1.0 / (d + e_up + e_now - e_up * ratio)
        ratio = e_now * inverse
        ratio_buf[k] = ratio
        new_values = []
        for c in range(4):
            val = (d * (q[c] + 0.1 * growth[c]) + e_up * values[c]) * inverse
            val_buf[c, k] = val
            new_values.append(val)
        return acc_x, acc_y, force_u, force_v, e_now, ratio, tuple(new_values)

    zero = jnp.zeros((8, 128), F32)
    carry = (zero, zero, zero, zero, zero, zero, (zero, zero, zero, zero))
    for n in range(CHUNKS):
        pl.when(has_s)(to_north[n].wait_recv)
        pl.when(has_n)(to_south[n].wait_recv)
        carry = lax.fori_loop(n * per_chunk, (n + 1) * per_chunk, level_body, carry)

    scale = land_f / safe
    push1[0] = carry[2] * scale
    push1[1] = carry[3] * scale
    push_copies = pair(push1, p2recv)
    for c in push_copies:
        c.start()

    def back_body(i, state):
        after, mean_u, mean_v = state
        k = levels - 1 - i
        ratio = ratio_buf[k]
        now = [val_buf[c, k] + ratio * after[c] for c in range(4)]
        val_buf[0, k] = now[0]
        val_buf[1, k] = now[1]
        trc_out[0, k] = now[2]
        trc_out[1, k] = now[3]
        part = jnp.where(k.astype(F32) < be, dz[k], 0.0)
        return tuple(now), mean_u + part * now[0], mean_v + part * now[1]

    half = levels // 4
    state = lax.fori_loop(0, half, back_body, ((zero,) * 4, zero, zero))
    for c in push_copies:
        c.wait_recv()
    for f in range(2):
        wide2[f, :, 0:128] = push1[f]
        wide2[f, :, 128:256] = jnp.where(lane < 64, p2recv[1, f], p2recv[0, f])
    starts2, waits2 = peers(wide2, all2)
    for c in starts2:
        c.start()
    all2[:, rows_of(t), :] = wide2[...]
    state = lax.fori_loop(half, levels, back_body, state)
    unused, mean_u, mean_v = state

    shape = (8 * tiles, 256)
    rows = lax.broadcasted_iota(jnp.int32, shape, 0)
    top, base = rows == shape[0] - 1, rows == 0
    sea = jnp.where(all1[3] >= 0.0, 1.0, 0.0)
    ratio_x = 0.05 * all1[4]
    for c in waits2:
        c.wait_recv()
    all1[3] = sea
    all1[4] = ratio_x
    all1[5] = 0.1 * all1[5] * sea
    all2[0] = 0.1 * all2[0] * sea
    all2[1] = 0.1 * all2[1] * sea
    mine = rows_of(t)

    def diff_x(a):
        return pltpu.roll(a, 255, 1) - pltpu.roll(a, 1, 1)

    def diff_y(a):
        return jnp.where(top, 0.0, pltpu.roll(a, shape[0] - 1, 0)) - jnp.where(
            base, 0.0, pltpu.roll(a, 1, 0)
        )

    def sub_body(i, sums):
        height, u, v = all1[0], all1[1], all1[2]
        sea, dr, f = all1[3], all1[4], all1[5]
        height = (height - (diff_x(dr * u) + diff_y(dr * v))) * sea
        g = 1.25 * sea
        new_u = u * sea + all2[0] + f * v - g * diff_x(height)
        new_v = v * sea + all2[1] - f * u - g * diff_y(height)
        all1[0] = height
        all1[1] = new_u
        all1[2] = new_v
        return sums[0] + all1[1, mine, 0:128], sums[1] + all1[2, mine, 0:128]

    sum_u, sum_v = lax.fori_loop(0, NSUB, sub_body, (zero, zero))
    surf_out[...] = all1[0, mine, 0:128]
    baro_out[0] = all1[1, mine, 0:128]
    baro_out[1] = all1[2, mine, 0:128]
    shift_u = sum_u * (1.0 / NSUB) - mean_u / safe
    shift_v = sum_v * (1.0 / NSUB) - mean_v / safe

    def out_body(k, carry):
        wet = k.astype(F32) < be
        vel_out[0, k] = jnp.where(wet, val_buf[0, k] + shift_u, 0.0)
        vel_out[1, k] = jnp.where(wet, val_buf[1, k] + shift_v, 0.0)
        return carry

    lax.fori_loop(0, levels, out_body, 0)

    for c in two_d + x_copies + starts1 + push_copies + starts2:
        c.wait_send()
    for c in to_north + diag_n:
        pl.when(has_n)(c.wait_send)
    for c in to_south + diag_s:
        pl.when(has_s)(c.wait_send)


def shards(nx, ngy, nga, velocity, tracers, mixing, thickness, coriolis, land, bottom, surface, barotropic):
    levels = thickness.shape[0]
    tiles = ngy * nga
    groups = (levels + 31) // 32
    copies = 2 + 2 * CHUNKS + 2 + 4 + (tiles - 1) + 2 + (tiles - 1)
    tile = (8, 128)
    scratch = [
        (levels,) + tile, (levels,) + tile, (levels,) + tile, (levels,) + tile,
        (6, groups) + tile, (2, 4, groups) + tile, (2, groups) + tile, (2, groups) + tile,
        (4, groups) + tile, (4, groups) + tile, (2, groups) + tile,
        (6,) + tile, (2, 6) + tile, (6, 8, 256), (6, 8 * tiles, 256),
        (2,) + tile, (2, 2) + tile, (2, 8, 256), (2, 8 * tiles, 256),
        (levels,) + tile, (4, levels) + tile,
    ]
    vmem = pl.BlockSpec(memory_space=pltpu.VMEM)
    smem = pl.BlockSpec(memory_space=pltpu.SMEM)
    return pl.pallas_call(
        functools.partial(kernel, nx, ngy, nga, levels),
        out_shape=(
            jax.ShapeDtypeStruct(velocity.shape, F32),
            jax.ShapeDtypeStruct(tracers.shape, F32),
            jax.ShapeDtypeStruct(surface.shape, F32),
            jax.ShapeDtypeStruct(barotropic.shape, F32),
        ),
        in_specs=[vmem, vmem, vmem, smem, smem, vmem, vmem, vmem, vmem],
        out_specs=(vmem, vmem, vmem, vmem),
        scratch_shapes=[pltpu.VMEM(s, F32) for s in scratch]
        + [pltpu.SemaphoreType.DMA((copies,)), pltpu.SemaphoreType.DMA((copies,))],
        compiler_params=pltpu.CompilerParams(
            collective_id=0, has_side_effects=True, vmem_limit_bytes=40 * 1024 * 1024
        ),
    )(velocity, tracers, mixing, thickness, coriolis, land, bottom, surface, barotropic)


def solution(mesh):
    sizes = mesh.shape
    return jax.shard_map(
        functools.partial(shards, sizes["gx"], sizes["gy"], sizes["ga"]),
        mesh=mesh,
        in_specs=(
            P(None, None, ("gy", "ga"), "gx"),
            P(None, None, ("gy", "ga"), "gx"),
            P(None, ("gy", "ga"), "gx"),
            P(),
            P(("gy", "ga")),
            P(("gy", "ga"), "gx"),
            P(("gy", "ga"), "gx"),
            P(("gy", "ga"), "gx"),
            P(None, ("gy", "ga"), "gx"),
        ),
        out_specs=(
            P(None, None, ("gy", "ga"), "gx"),
            P(None, None, ("gy", "ga"), "gx"),
            P(("gy", "ga"), "gx"),
            P(None, ("gy", "ga"), "gx"),
        ),
        check_vma=False,
    )
```

```python
import functools
import jax
import jax.numpy as jnp
from jax import lax
from jax.experimental import pallas as pl
from jax.experimental.pallas import tpu as pltpu
from jax.sharding import PartitionSpec as P

NSUB = 30
F32 = jnp.float32
MESH = pl.DeviceIdType.MESH
BLOCK = 8


def kernel(
    nx, ngy, nga, levels,
    vel_in, trc_in, mix_in, dz_in, cor_in, land_in, bot_in, surf_in, baro_in,
    vel_out, trc_out, surf_out, baro_out,
    ynorth, ysouth, hnorth, hsouth,
    xpack, xrecv, crn, crs, bq, bl, bcorn,
    tile2, t2recv, wide1, all1, push1, p2recv, wide2, all2,
    ratio_buf, val_buf, be_above, be_below,
    vel, trc, mix, dz, cor, land, bot, surf, baro,
    send_sem, recv_sem, load_sem,
):
    tiles = ngy * nga
    groups = xpack.shape[1]
    blocks = levels // BLOCK
    per_group = 32 // BLOCK
    loads = [
        pltpu.make_async_copy(src, dst, load_sem.at[i])
        for i, (src, dst) in enumerate([
            (dz_in, dz), (cor_in, cor), (land_in, land), (bot_in, bot), (surf_in, surf),
            (baro_in, baro), (vel_in, vel), (trc_in, trc), (mix_in, mix),
        ])
    ]
    for c in loads:
        c.start()
    gx = lax.axis_index("gx")
    t = lax.axis_index("gy") * nga + lax.axis_index("ga")
    left = lax.rem(gx + nx - 1, nx)
    right = lax.rem(gx + 1, nx)
    has_n = t < tiles - 1
    has_s = t > 0

    def dev(x, tile):
        return {"gx": x, "gy": tile // nga, "ga": lax.rem(tile, nga)}

    up = jnp.minimum(t + 1, tiles - 1)
    down = jnp.maximum(t - 1, 0)

    barrier = pltpu.get_barrier_semaphore()

    def greet(d):
        pl.semaphore_signal(barrier, inc=1, device_id=d, device_id_type=MESH)

    greet(dev(left, t))
    greet(dev(right, t))
    for p in range(1, tiles):
        greet(dev(gx, lax.rem(t + p, tiles)))

    @pl.when(has_n)
    def _():
        greet(dev(left, up))
        greet(dev(right, up))

    @pl.when(has_s)
    def _():
        greet(dev(left, down))
        greet(dev(right, down))

    row = lax.broadcasted_iota(jnp.int32, (8, 128), 0)
    lane = lax.broadcasted_iota(jnp.int32, (8, 128), 1)
    slot = lane // 4
    l4 = lane - 4 * slot
    first_l, last_l = lane == 0, lane == 127
    first_r, last_r = row == 0, row == 7

    for c in loads[:6]:
        c.wait()
    land_i = land[...]
    be = jnp.where(land_i > 0, bot[...], -1).astype(F32)
    land_f = land_i.astype(F32)

    def depth_body(n, acc):
        total, depth = acc
        for i in range(BLOCK):
            k = n * BLOCK + i
            d = dz[k]
            total = total + d
            depth = depth + jnp.where(k.astype(F32) < be, d, 0.0)
        return total, depth

    dz_total, depth_sum = lax.fori_loop(
        0, blocks, depth_body, (jnp.float32(0.0), jnp.zeros((8, 128), F32))
    )
    safe = jnp.maximum(depth_sum, 1.0)
    rot = jnp.zeros((8, 128), F32)
    for r in range(8):
        rot = jnp.where(row == r, cor[r], rot)
    tile2[0] = surf[...]
    tile2[1] = baro[0]
    tile2[2] = baro[1]
    tile2[3] = be
    tile2[4] = depth_sum / jnp.broadcast_to(dz_total, (8, 128))
    tile2[5] = rot

    pl.semaphore_wait(
        barrier, 2 + tiles - 1 + jnp.where(has_n, 2, 0) + jnp.where(has_s, 2, 0)
    )

    def rc(src, dst, i, d):
        return pltpu.make_async_remote_copy(
            src_ref=src, dst_ref=dst, send_sem=send_sem.at[i], recv_sem=recv_sem.at[i],
            device_id=d, device_id_type=MESH,
        )

    index = [0]

    def nxt():
        index[0] += 1
        return index[0] - 1

    def rows_of(tile):
        return pl.ds(pl.multiple_of(tile * 8, 8), 8)

    def pair(src, recv):
        return [
            rc(src, recv.at[0], nxt(), dev(right, t)),
            rc(src, recv.at[1], nxt(), dev(left, t)),
        ]

    def peers(src, dst):
        starts, waits = [], []
        for p in range(1, tiles):
            i = nxt()
            to = lax.rem(t + p, tiles)
            origin = lax.rem(t + tiles - p, tiles)
            starts.append(rc(src, dst.at[:, rows_of(t), :], i, dev(gx, to)))
            waits.append(rc(src, dst.at[:, rows_of(origin), :], i, dev(gx, to)))
        return starts, waits

    two_d = pair(tile2, t2recv)
    for c in two_d:
        c.start()
    be_up = rc(tile2.at[3], be_below, nxt(), dev(gx, up))
    be_down = rc(tile2.at[3], be_above, nxt(), dev(gx, down))
    pl.when(has_n)(be_up.start)
    pl.when(has_s)(be_down.start)
    for c in loads[6:8]:
        c.wait()

    @pl.when(jnp.logical_not(has_n))
    def _():
        hnorth[...] = jnp.zeros_like(hnorth)
        crn[...] = jnp.zeros_like(crn)
        be_above[...] = jnp.full_like(be_above, -1.0)

    @pl.when(jnp.logical_not(has_s))
    def _():
        hsouth[...] = jnp.zeros_like(hsouth)
        crs[...] = jnp.zeros_like(crs)
        be_below[...] = jnp.full_like(be_below, -1.0)

    xpack[...] = jnp.zeros_like(xpack)

    def field(c, k):
        return vel[c, k] if c < 2 else trc[c - 2, k]

    def pack_body(n, carry):
        acc = [jnp.zeros((8, 128), F32)] * 6
        for i in range(BLOCK):
            k = n * BLOCK + i
            wet = k.astype(F32) < be
            q = [jnp.where(wet, field(c, k), 0.0) for c in range(4)]
            yn = jnp.concatenate([a[6:8] for a in q], axis=0)
            ys = jnp.concatenate([a[0:2] for a in q], axis=0)
            ynorth[k] = yn
            ysouth[k] = ys
            here = slot == i
            for c, a in enumerate(q + [yn, ys]):
                acc[c] = jnp.where(here, pltpu.roll(a, 2 + 4 * i, 1), acc[c])
        g = n // per_group
        part = n - per_group * g
        here = slot // BLOCK == part
        for c in range(6):
            xpack[c, g] = jnp.where(
                here, pltpu.roll(acc[c], 4 * BLOCK * part, 1), xpack[c, g]
            )
        return carry

    lax.fori_loop(0, blocks, pack_body, 0)
    x_copies = pair(xpack.at[pl.ds(0, 4)], xrecv)
    for c in x_copies:
        c.start()
    diag_n = [
        rc(xpack.at[4], crs.at[1], nxt(), dev(left, up)),
        rc(xpack.at[4], crs.at[0], nxt(), dev(right, up)),
    ]
    diag_s = [
        rc(xpack.at[5], crn.at[1], nxt(), dev(left, down)),
        rc(xpack.at[5], crn.at[0], nxt(), dev(right, down)),
    ]
    for c in diag_n:
        pl.when(has_n)(c.start)
    for c in diag_s:
        pl.when(has_s)(c.start)

    first_north, first_south = index[0], index[0] + blocks
    index[0] += 2 * blocks

    def to_north(n):
        span = pl.ds(n * BLOCK, BLOCK)
        return rc(ynorth.at[span], hsouth.at[span], first_north + n, dev(gx, up))

    def to_south(n):
        span = pl.ds(n * BLOCK, BLOCK)
        return rc(ysouth.at[span], hnorth.at[span], first_south + n, dev(gx, down))

    for n in range(blocks):
        pl.when(has_n)(to_north(n).start)
        pl.when(has_s)(to_south(n).start)

    for c in two_d:
        c.wait_recv()
    for f in range(6):
        wide1[f, :, 0:128] = tile2[f]
        wide1[f, :, 128:256] = jnp.where(lane < 64, t2recv[1, f], t2recv[0, f])
    starts1, waits1 = peers(wide1, all1)
    for c in starts1:
        c.start()
    all1[:, rows_of(t), :] = wide1[...]

    be_side = jnp.where(
        l4 == 1,
        jnp.broadcast_to(t2recv[0, 3][:, 127:128], (8, 128)),
        jnp.broadcast_to(t2recv[1, 3][:, 0:1], (8, 128)),
    )
    for c in x_copies:
        c.wait_recv()
    for c in diag_n:
        pl.when(has_s)(c.wait_recv)
    for c in diag_s:
        pl.when(has_n)(c.wait_recv)

    def close(a):
        return jnp.where(l4 == 1, a, pltpu.roll(a, 126, 1))

    low = l4 < 2
    for g in range(groups):
        corner_n = jnp.where(low, crn[0, g], crn[1, g])
        corner_s = jnp.where(low, crs[0, g], crs[1, g])
        bcorn[0, g] = close(corner_n)
        bcorn[1, g] = close(corner_s)
        wet = (32 * g + slot).astype(F32) < be_side
        for c in range(4):
            a = jnp.where(low, xrecv[0, c, g], xrecv[1, c, g])
            mine = xpack[c, g]
            sides = jnp.where(
                l4 == 1,
                pltpu.roll(a, 1, 1) + pltpu.roll(mine, 127, 1),
                pltpu.roll(a, 127, 1) + pltpu.roll(mine, 1, 1),
            )
            north = jnp.where(
                last_r, jnp.broadcast_to(corner_n[2 * c:2 * c + 1], (8, 128)), pltpu.roll(a, 7, 0)
            )
            south = jnp.where(
                first_r, jnp.broadcast_to(corner_s[2 * c + 1:2 * c + 2], (8, 128)), pltpu.roll(a, 1, 0)
            )
            lap = jnp.where(wet, sides + north + south - 4.0 * a, 0.0)
            bq[c, g] = close(a)
            bl[c, g] = close(lap)

    pl.when(has_s)(be_up.wait_recv)
    pl.when(has_n)(be_down.wait_recv)
    loads[8].wait()
    be_n = jnp.broadcast_to(be_above[0:1, :], (8, 128))
    be_s = jnp.broadcast_to(be_below[7:8, :], (8, 128))

    def east_west(a, h):
        return (
            jnp.where(last_l, h, pltpu.roll(a, 127, 1)),
            jnp.where(first_l, h, pltpu.roll(a, 1, 1)),
        )

    def row_of(a, r):
        return jnp.broadcast_to(a[r:r + 1], (8, 128))

    def level(n, i, rims, carry):
        rim_q, rim_l, rim_c = rims
        k = n * BLOCK + i
        acc_x, acc_y, force_u, force_v, e_up, ratio, values = carry
        kf = k.astype(F32)
        d = dz[k]
        k_next = jnp.minimum(k + 1, levels - 1)
        d_next = dz[k_next]
        turn = 127 - 4 * i
        wet = kf < be
        wet_next = jnp.logical_and(kf + 1.0 < be, k + 1 < levels)
        q = [jnp.where(wet, field(c, k), 0.0) for c in range(4)]
        hn, hs = hnorth[k], hsouth[k]
        he, hw = east_west(hn, pltpu.roll(rim_c[0], turn, 1))
        lap_n = jnp.where(
            kf < be_n, pltpu.roll(hn + ynorth[k], 7, 0) + he + hw - 4.0 * hn, 0.0
        )
        he, hw = east_west(hs, pltpu.roll(rim_c[1], turn, 1))
        lap_s = jnp.where(
            kf < be_s, pltpu.roll(hs + ysouth[k], 1, 0) + he + hw - 4.0 * hs, 0.0
        )
        around, smooth = [], []
        for c in range(4):
            a = q[c]
            e, w = east_west(a, pltpu.roll(rim_q[c], turn, 1))
            n = jnp.where(last_r, jnp.broadcast_to(hnorth[k, 2 * c:2 * c + 1, :], (8, 128)), pltpu.roll(a, 7, 0))
            s = jnp.where(first_r, jnp.broadcast_to(hsouth[k, 2 * c + 1:2 * c + 2, :], (8, 128)), pltpu.roll(a, 1, 0))
            around.append((e, w, n, s))
            lap = jnp.where(wet, (e + w) + (n + s) - 4.0 * a, 0.0)
            e, w = east_west(lap, pltpu.roll(rim_l[c], turn, 1))
            n = jnp.where(last_r, row_of(lap_n, 2 * c), pltpu.roll(lap, 7, 0))
            s = jnp.where(first_r, row_of(lap_s, 2 * c + 1), pltpu.roll(lap, 1, 0))
            smooth.append(0.02 * ((e + w) + (n + s) - 4.0 * lap))
        weights = [
            (0.1 * around[3][i] - 0.2 * around[2][i]) * d for i in range(4)
        ]
        slope_x = weights[0] - weights[1]
        slope_y = weights[2] - weights[3]
        press_x = 0.01 * (acc_x + 0.5 * slope_x)
        press_y = 0.01 * (acc_y + 0.5 * slope_y)
        acc_x = acc_x + slope_x
        acc_y = acc_y + slope_y
        ue, uw = around[0][0], around[0][1]
        vn, vs = around[1][2], around[1][3]
        extra = [rot * q[1] - press_x, -rot * q[0] - press_y, 0.0, 0.0]
        growth = []
        for c in range(4):
            e, w, n, s = around[c]
            advect = 0.5 * ((ue * e - uw * w) + (vn * n - vs * s))
            growth.append(jnp.where(wet, extra[c] - smooth[c] - advect, 0.0))
        force_u = force_u + d * growth[0]
        force_v = force_v + d * growth[1]
        e_now = jnp.where(
            jnp.logical_and(wet, wet_next), mix[k] / (0.5 * (d + d_next)), 0.0
        )
        inverse = 1.0 / (d + e_up + e_now - e_up * ratio)
        ratio = e_now * inverse
        ratio_buf[k] = ratio
        new_values = []
        for c in range(4):
            val = (d * (q[c] + 0.1 * growth[c]) + e_up * values[c]) * inverse
            val_buf[c, k] = val
            new_values.append(val)
        return acc_x, acc_y, force_u, force_v, e_now, ratio, tuple(new_values)

    zero = jnp.zeros((8, 128), F32)
    carry = (zero, zero, zero, zero, zero, zero, (zero, zero, zero, zero))

    def block_body(n, carry):
        g = n // per_group
        back = lax.rem(128 - 4 * BLOCK * (n - per_group * g), 128)
        rims = (
            [pltpu.roll(bq[c, g], back, 1) for c in range(4)],
            [pltpu.roll(bl[c, g], back, 1) for c in range(4)],
            [pltpu.roll(bcorn[c, g], back, 1) for c in range(2)],
        )
        pl.when(has_s)(lambda: to_north(n).wait_recv())
        pl.when(has_n)(lambda: to_south(n).wait_recv())
        for i in range(BLOCK):
            carry = level(n, i, rims, carry)
        return carry

    carry = lax.fori_loop(0, blocks, block_body, carry)

    scale = land_f / safe
    push1[0] = carry[2] * scale
    push1[1] = carry[3] * scale
    push_copies = pair(push1, p2recv)
    for c in push_copies:
        c.start()

    def back_body(n, state):
        after, mean_u, mean_v = state
        for i in range(BLOCK):
            k = levels - 1 - n * BLOCK - i
            ratio = ratio_buf[k]
            now = [val_buf[c, k] + ratio * after[c] for c in range(4)]
            val_buf[0, k] = now[0]
            val_buf[1, k] = now[1]
            trc_out[0, k] = now[2]
            trc_out[1, k] = now[3]
            part = jnp.where(k.astype(F32) < be, dz[k], 0.0)
            mean_u = mean_u + part * now[0]
            mean_v = mean_v + part * now[1]
            after = tuple(now)
        return after, mean_u, mean_v

    half = blocks // 3
    state = lax.fori_loop(0, half, back_body, ((zero,) * 4, zero, zero))
    for c in push_copies:
        c.wait_recv()
    for f in range(2):
        wide2[f, :, 0:128] = push1[f]
        wide2[f, :, 128:256] = jnp.where(lane < 64, p2recv[1, f], p2recv[0, f])
    starts2, waits2 = peers(wide2, all2)
    for c in starts2:
        c.start()
    all2[:, rows_of(t), :] = wide2[...]
    state = lax.fori_loop(half, blocks, back_body, state)
    unused, mean_u, mean_v = state

    shape = (8 * tiles, 256)
    rows = lax.broadcasted_iota(jnp.int32, shape, 0)
    top, base = rows == shape[0] - 1, rows == 0
    for c in waits1:
        c.wait_recv()
    sea = jnp.where(all1[3] >= 0.0, 1.0, 0.0)
    ratio_x = 0.05 * all1[4]
    for c in waits2:
        c.wait_recv()
    all1[3] = sea
    all1[4] = ratio_x
    all1[5] = 0.1 * all1[5] * sea
    all2[0] = 0.1 * all2[0] * sea
    all2[1] = 0.1 * all2[1] * sea
    mine = rows_of(t)

    def diff_x(a):
        return pltpu.roll(a, 255, 1) - pltpu.roll(a, 1, 1)

    def diff_y(a):
        return jnp.where(top, 0.0, pltpu.roll(a, shape[0] - 1, 0)) - jnp.where(
            base, 0.0, pltpu.roll(a, 1, 0)
        )

    def sub_body(i, sums):
        height, u, v = all1[0], all1[1], all1[2]
        sea, dr, f = all1[3], all1[4], all1[5]
        height = (height - (diff_x(dr * u) + diff_y(dr * v))) * sea
        g = 1.25 * sea
        new_u = u * sea + all2[0] + f * v - g * diff_x(height)
        new_v = v * sea + all2[1] - f * u - g * diff_y(height)
        all1[0] = height
        all1[1] = new_u
        all1[2] = new_v
        return sums[0] + all1[1, mine, 0:128], sums[1] + all1[2, mine, 0:128]

    sum_u, sum_v = lax.fori_loop(0, NSUB, sub_body, (zero, zero))
    surf_out[...] = all1[0, mine, 0:128]
    baro_out[0] = all1[1, mine, 0:128]
    baro_out[1] = all1[2, mine, 0:128]
    shift_u = sum_u * (1.0 / NSUB) - mean_u / safe
    shift_v = sum_v * (1.0 / NSUB) - mean_v / safe

    def out_body(n, carry):
        for i in range(BLOCK):
            k = n * BLOCK + i
            wet = k.astype(F32) < be
            vel_out[0, k] = jnp.where(wet, val_buf[0, k] + shift_u, 0.0)
            vel_out[1, k] = jnp.where(wet, val_buf[1, k] + shift_v, 0.0)
        return carry

    lax.fori_loop(0, blocks, out_body, 0)

    for c in two_d + x_copies + starts1 + push_copies + starts2:
        c.wait_send()
    norths = diag_n + [be_up] + [to_north(n) for n in range(blocks)]
    souths = diag_s + [be_down] + [to_south(n) for n in range(blocks)]
    for c in norths:
        pl.when(has_n)(c.wait_send)
    for c in souths:
        pl.when(has_s)(c.wait_send)


def settle(*refs):
    count = len(refs) // 2
    sem = refs[-1]
    copies = [pltpu.make_async_copy(refs[i], refs[count + i], sem.at[i]) for i in range(count)]
    for c in copies:
        c.start()
    for c in copies:
        c.wait()


def shards(nx, ngy, nga, velocity, tracers, mixing, thickness, coriolis, land, bottom, surface, barotropic):
    levels = thickness.shape[0]
    tiles = ngy * nga
    groups = (levels + 31) // 32
    copies = 4 + 2 * (levels // BLOCK) + 2 + 4 + (tiles - 1) + 2 + (tiles - 1)
    tile = (8, 128)
    scratch = [
        (levels,) + tile, (levels,) + tile, (levels,) + tile, (levels,) + tile,
        (6, groups) + tile, (2, 4, groups) + tile, (2, groups) + tile, (2, groups) + tile,
        (4, groups) + tile, (4, groups) + tile, (2, groups) + tile,
        (6,) + tile, (2, 6) + tile, (6, 8, 256), (6, 8 * tiles, 256),
        (2,) + tile, (2, 2) + tile, (2, 8, 256), (2, 8 * tiles, 256),
        (levels,) + tile, (4, levels) + tile, tile, tile,
    ]
    staged = [
        pltpu.VMEM(velocity.shape, F32), pltpu.VMEM(tracers.shape, F32), pltpu.VMEM(mixing.shape, F32),
        pltpu.SMEM(thickness.shape, F32), pltpu.SMEM(coriolis.shape, F32),
        pltpu.VMEM(land.shape, jnp.int32), pltpu.VMEM(bottom.shape, jnp.int32),
        pltpu.VMEM(surface.shape, F32), pltpu.VMEM(barotropic.shape, F32),
    ]
    vmem = pl.BlockSpec(memory_space=pltpu.VMEM)
    far = pl.BlockSpec(memory_space=pltpu.HBM)
    results = pl.pallas_call(
        functools.partial(kernel, nx, ngy, nga, levels),
        out_shape=(
            jax.ShapeDtypeStruct(velocity.shape, F32),
            jax.ShapeDtypeStruct(tracers.shape, F32),
            jax.ShapeDtypeStruct(surface.shape, F32),
            jax.ShapeDtypeStruct(barotropic.shape, F32),
        ),
        in_specs=[far] * 9,
        out_specs=(vmem, vmem, vmem, vmem),
        scratch_shapes=[pltpu.VMEM(s, F32) for s in scratch]
        + staged
        + [pltpu.SemaphoreType.DMA((copies,)), pltpu.SemaphoreType.DMA((copies,)), pltpu.SemaphoreType.DMA((9,))],
        compiler_params=pltpu.CompilerParams(
            collective_id=0, has_side_effects=True, vmem_limit_bytes=64 * 1024 * 1024
        ),
    )(velocity, tracers, mixing, thickness, coriolis, land, bottom, surface, barotropic)
    anywhere = pl.BlockSpec(memory_space=pltpu.HBM)
    return pl.pallas_call(
        settle,
        out_shape=tuple(jax.ShapeDtypeStruct(r.shape, r.dtype) for r in results),
        in_specs=[anywhere] * 4,
        out_specs=(anywhere,) * 4,
        scratch_shapes=[pltpu.SemaphoreType.DMA((4,))],
        compiler_params=pltpu.CompilerParams(vmem_limit_bytes=64 * 1024 * 1024),
    )(*results)


def solution(mesh):
    sizes = mesh.shape
    return jax.shard_map(
        functools.partial(shards, sizes["gx"], sizes["gy"], sizes["ga"]),
        mesh=mesh,
        in_specs=(
            P(None, None, ("gy", "ga"), "gx"),
            P(None, None, ("gy", "ga"), "gx"),
            P(None, ("gy", "ga"), "gx"),
            P(),
            P(("gy", "ga")),
            P(("gy", "ga"), "gx"),
            P(("gy", "ga"), "gx"),
            P(("gy", "ga"), "gx"),
            P(None, ("gy", "ga"), "gx"),
        ),
        out_specs=(
            P(None, None, ("gy", "ga"), "gx"),
            P(None, None, ("gy", "ga"), "gx"),
            P(("gy", "ga"), "gx"),
            P(None, ("gy", "ga"), "gx"),
        ),
        check_vma=False,
    )
```

```python
import functools
import jax
import jax.numpy as jnp
from jax import lax
from jax.experimental import pallas as pl
from jax.experimental.pallas import tpu as pltpu
from jax.sharding import PartitionSpec as P

NSUB = 30
F32 = jnp.float32
MESH = pl.DeviceIdType.MESH
BLOCK = 8


def kernel(
    nx, ngy, nga, levels,
    vel_in, trc_in, mix_in, dz_in, cor_in, land_in, bot_in, surf_in, baro_in,
    vel_out, trc_out, surf_out, baro_out,
    ynorth, ysouth, hnorth, hsouth,
    xpack, xrecv, crn, crs, bq, bl, bcorn,
    tile2, t2recv, wide1, all1, push1, p2recv, wide2, all2,
    ratio_buf, val_buf, be_above, be_below, state, fixed, high, flow,
    vel, trc, mix, dz, cor, land, bot, surf, baro,
    send_sem, recv_sem, load_sem,
):
    tiles = ngy * nga
    groups = xpack.shape[1]
    blocks = levels // BLOCK
    per_group = 32 // BLOCK
    loads = [
        pltpu.make_async_copy(src, dst, load_sem.at[i])
        for i, (src, dst) in enumerate([
            (dz_in, dz), (cor_in, cor), (land_in, land), (bot_in, bot), (surf_in, surf),
            (baro_in, baro), (vel_in, vel), (trc_in, trc), (mix_in, mix),
        ])
    ]
    for c in loads:
        c.start()
    gx = lax.axis_index("gx")
    t = lax.axis_index("gy") * nga + lax.axis_index("ga")
    left = lax.rem(gx + nx - 1, nx)
    right = lax.rem(gx + 1, nx)
    has_n = t < tiles - 1
    has_s = t > 0

    def dev(x, tile):
        return {"gx": x, "gy": tile // nga, "ga": lax.rem(tile, nga)}

    up = jnp.minimum(t + 1, tiles - 1)
    down = jnp.maximum(t - 1, 0)

    barrier = pltpu.get_barrier_semaphore()

    def greet(d):
        pl.semaphore_signal(barrier, inc=1, device_id=d, device_id_type=MESH)

    greet(dev(left, t))
    greet(dev(right, t))
    for p in range(1, tiles):
        greet(dev(gx, lax.rem(t + p, tiles)))

    @pl.when(has_n)
    def _():
        greet(dev(left, up))
        greet(dev(right, up))

    @pl.when(has_s)
    def _():
        greet(dev(left, down))
        greet(dev(right, down))

    row = lax.broadcasted_iota(jnp.int32, (8, 128), 0)
    lane = lax.broadcasted_iota(jnp.int32, (8, 128), 1)
    slot = lane // 4
    l4 = lane - 4 * slot
    first_l, last_l = lane == 0, lane == 127
    first_r, last_r = row == 0, row == 7

    for c in loads[:6]:
        c.wait()
    land_i = land[...]
    be = jnp.where(land_i > 0, bot[...], -1).astype(F32)
    land_f = land_i.astype(F32)

    def depth_body(n, acc):
        total, depth = acc
        for i in range(BLOCK):
            k = n * BLOCK + i
            d = dz[k]
            total = total + d
            depth = depth + jnp.where(k.astype(F32) < be, d, 0.0)
        return total, depth

    dz_total, depth_sum = lax.fori_loop(
        0, blocks, depth_body, (jnp.float32(0.0), jnp.zeros((8, 128), F32))
    )
    safe = jnp.maximum(depth_sum, 1.0)
    rot = jnp.zeros((8, 128), F32)
    for r in range(8):
        rot = jnp.where(row == r, cor[r], rot)
    tile2[0] = surf[...]
    tile2[1] = baro[0]
    tile2[2] = baro[1]
    tile2[3] = depth_sum / jnp.broadcast_to(dz_total, (8, 128))
    tile2[4] = be

    pl.semaphore_wait(
        barrier, 2 + tiles - 1 + jnp.where(has_n, 2, 0) + jnp.where(has_s, 2, 0)
    )

    def rc(src, dst, i, d):
        return pltpu.make_async_remote_copy(
            src_ref=src, dst_ref=dst, send_sem=send_sem.at[i], recv_sem=recv_sem.at[i],
            device_id=d, device_id_type=MESH,
        )

    index = [0]

    def nxt():
        index[0] += 1
        return index[0] - 1

    def rows_of(tile):
        return pl.ds(pl.multiple_of(tile * 8, 8), 8)

    def pair(src, recv):
        return [
            rc(src, recv.at[0], nxt(), dev(right, t)),
            rc(src, recv.at[1], nxt(), dev(left, t)),
        ]

    def peers(src, dst):
        starts, waits = [], []
        for p in range(1, tiles):
            i = nxt()
            to = lax.rem(t + p, tiles)
            origin = lax.rem(t + tiles - p, tiles)
            starts.append(rc(src, dst.at[t], i, dev(gx, to)))
            waits.append(rc(src, dst.at[origin], i, dev(gx, to)))
        return starts, waits

    two_d = pair(tile2, t2recv)
    for c in two_d:
        c.start()
    be_up = rc(tile2.at[4], be_below, nxt(), dev(gx, up))
    be_down = rc(tile2.at[4], be_above, nxt(), dev(gx, down))
    pl.when(has_n)(be_up.start)
    pl.when(has_s)(be_down.start)
    for c in loads[6:8]:
        c.wait()

    @pl.when(jnp.logical_not(has_n))
    def _():
        hnorth[...] = jnp.zeros_like(hnorth)
        crn[...] = jnp.zeros_like(crn)
        be_above[...] = jnp.full_like(be_above, -1.0)

    @pl.when(jnp.logical_not(has_s))
    def _():
        hsouth[...] = jnp.zeros_like(hsouth)
        crs[...] = jnp.zeros_like(crs)
        be_below[...] = jnp.full_like(be_below, -1.0)

    xpack[...] = jnp.zeros_like(xpack)

    def field(c, k):
        return vel[c, k] if c < 2 else trc[c - 2, k]

    def masked(k):
        wet = k.astype(F32) < be
        return [jnp.where(wet, field(c, k), 0.0) for c in range(4)]

    def place(n, first, acc):
        g = n // per_group
        part = n - per_group * g
        here = slot // BLOCK == part
        for j, a in enumerate(acc):
            xpack[first + j, g] = jnp.where(
                here, pltpu.roll(a, 4 * BLOCK * part, 1), xpack[first + j, g]
            )

    def pack_rows(n, carry):
        acc = [jnp.zeros((8, 128), F32)] * 2
        for i in range(BLOCK):
            k = n * BLOCK + i
            q = masked(k)
            ends = [
                jnp.concatenate([a[6:8] for a in q], axis=0),
                jnp.concatenate([a[0:2] for a in q], axis=0),
            ]
            ynorth[k] = ends[0]
            ysouth[k] = ends[1]
            for c in range(2):
                acc[c] = jnp.where(slot == i, pltpu.roll(ends[c], 2 + 4 * i, 1), acc[c])
        place(n, 4, acc)
        return carry

    def pack_columns(n, carry):
        acc = [jnp.zeros((8, 128), F32)] * 4
        for i in range(BLOCK):
            q = masked(n * BLOCK + i)
            for c in range(4):
                acc[c] = jnp.where(slot == i, pltpu.roll(q[c], 2 + 4 * i, 1), acc[c])
        place(n, 0, acc)
        return carry

    lax.fori_loop(0, blocks, pack_rows, 0)
    diag_n = [
        rc(xpack.at[4], crs.at[1], nxt(), dev(left, up)),
        rc(xpack.at[4], crs.at[0], nxt(), dev(right, up)),
    ]
    diag_s = [
        rc(xpack.at[5], crn.at[1], nxt(), dev(left, down)),
        rc(xpack.at[5], crn.at[0], nxt(), dev(right, down)),
    ]
    for c in diag_n:
        pl.when(has_n)(c.start)
    for c in diag_s:
        pl.when(has_s)(c.start)

    first_north, first_south = index[0], index[0] + blocks
    index[0] += 2 * blocks

    def to_north(n):
        span = pl.ds(n * BLOCK, BLOCK)
        return rc(ynorth.at[span], hsouth.at[span], first_north + n, dev(gx, up))

    def to_south(n):
        span = pl.ds(n * BLOCK, BLOCK)
        return rc(ysouth.at[span], hnorth.at[span], first_south + n, dev(gx, down))

    for n in range(blocks):
        pl.when(has_n)(to_north(n).start)
        pl.when(has_s)(to_south(n).start)

    lax.fori_loop(0, blocks, pack_columns, 0)
    x_copies = pair(xpack.at[pl.ds(0, 4)], xrecv)
    for c in x_copies:
        c.start()

    for c in two_d:
        c.wait_recv()
    for f in range(4):
        wide1[2 * f] = tile2[f]
        wide1[2 * f + 1] = jnp.where(lane < 64, t2recv[1, f], t2recv[0, f])
    wide1[8] = rot
    all1[t] = wide1[...]
    core = lax.rem(t // nga, 2)
    stride = 2 * nga
    chips = tiles // 2
    my_chip = (t // stride) * nga + lax.rem(t, nga)

    def tile_of(chip, on):
        return (chip // nga) * stride + on * nga + lax.rem(chip, nga)

    starts1, waits1 = [], []
    for p in range(1, chips):
        i = nxt()
        to = dev(gx, tile_of(lax.rem(my_chip + p, chips), core))
        origin = tile_of(lax.rem(my_chip + chips - p, chips), core)
        starts1.append(rc(wide1, all1.at[t], i, to))
        waits1.append(rc(wide1, all1.at[origin], i, to))
    for c in starts1:
        c.start()

    be_side = jnp.where(
        l4 == 1,
        jnp.broadcast_to(t2recv[0, 4][:, 127:128], (8, 128)),
        jnp.broadcast_to(t2recv[1, 4][:, 0:1], (8, 128)),
    )
    for c in x_copies:
        c.wait_recv()
    for c in diag_n:
        pl.when(has_s)(c.wait_recv)
    for c in diag_s:
        pl.when(has_n)(c.wait_recv)

    def close(a):
        return jnp.where(l4 == 1, a, pltpu.roll(a, 126, 1))

    low = l4 < 2
    for g in range(groups):
        corner_n = jnp.where(low, crn[0, g], crn[1, g])
        corner_s = jnp.where(low, crs[0, g], crs[1, g])
        bcorn[0, g] = close(corner_n)
        bcorn[1, g] = close(corner_s)
        wet = (32 * g + slot).astype(F32) < be_side
        for c in range(4):
            a = jnp.where(low, xrecv[0, c, g], xrecv[1, c, g])
            mine = xpack[c, g]
            sides = jnp.where(
                l4 == 1,
                pltpu.roll(a, 1, 1) + pltpu.roll(mine, 127, 1),
                pltpu.roll(a, 127, 1) + pltpu.roll(mine, 1, 1),
            )
            north = jnp.where(
                last_r, jnp.broadcast_to(corner_n[2 * c:2 * c + 1], (8, 128)), pltpu.roll(a, 7, 0)
            )
            south = jnp.where(
                first_r, jnp.broadcast_to(corner_s[2 * c + 1:2 * c + 2], (8, 128)), pltpu.roll(a, 1, 0)
            )
            lap = jnp.where(wet, sides + north + south - 4.0 * a, 0.0)
            bq[c, g] = close(a)
            bl[c, g] = close(lap)

    pl.when(has_s)(be_up.wait_recv)
    pl.when(has_n)(be_down.wait_recv)
    loads[8].wait()
    be_n = jnp.broadcast_to(be_above[0:1, :], (8, 128))
    be_s = jnp.broadcast_to(be_below[7:8, :], (8, 128))

    def east_west(a, h):
        return (
            jnp.where(last_l, h, pltpu.roll(a, 127, 1)),
            jnp.where(first_l, h, pltpu.roll(a, 1, 1)),
        )

    def row_of(a, r):
        return jnp.broadcast_to(a[r:r + 1], (8, 128))

    def level(n, i, rims, carry):
        rim_q, rim_l, rim_c = rims
        k = n * BLOCK + i
        acc_x, acc_y, force_u, force_v, e_up, ratio, values = carry
        kf = k.astype(F32)
        d = dz[k]
        k_next = jnp.minimum(k + 1, levels - 1)
        d_next = dz[k_next]
        turn = 127 - 4 * i
        wet = kf < be
        wet_next = jnp.logical_and(kf + 1.0 < be, k + 1 < levels)
        q = [jnp.where(wet, field(c, k), 0.0) for c in range(4)]
        hn, hs = hnorth[k], hsouth[k]
        he, hw = east_west(hn, pltpu.roll(rim_c[0], turn, 1))
        lap_n = jnp.where(
            kf < be_n, pltpu.roll(hn + ynorth[k], 7, 0) + he + hw - 4.0 * hn, 0.0
        )
        he, hw = east_west(hs, pltpu.roll(rim_c[1], turn, 1))
        lap_s = jnp.where(
            kf < be_s, pltpu.roll(hs + ysouth[k], 1, 0) + he + hw - 4.0 * hs, 0.0
        )
        around, smooth = [], []
        for c in range(4):
            a = q[c]
            e, w = east_west(a, pltpu.roll(rim_q[c], turn, 1))
            n = jnp.where(last_r, jnp.broadcast_to(hnorth[k, 2 * c:2 * c + 1, :], (8, 128)), pltpu.roll(a, 7, 0))
            s = jnp.where(first_r, jnp.broadcast_to(hsouth[k, 2 * c + 1:2 * c + 2, :], (8, 128)), pltpu.roll(a, 1, 0))
            around.append((e, w, n, s))
            lap = jnp.where(wet, (e + w) + (n + s) - 4.0 * a, 0.0)
            e, w = east_west(lap, pltpu.roll(rim_l[c], turn, 1))
            n = jnp.where(last_r, row_of(lap_n, 2 * c), pltpu.roll(lap, 7, 0))
            s = jnp.where(first_r, row_of(lap_s, 2 * c + 1), pltpu.roll(lap, 1, 0))
            smooth.append(0.02 * ((e + w) + (n + s) - 4.0 * lap))
        weights = [
            (0.1 * around[3][i] - 0.2 * around[2][i]) * d for i in range(4)
        ]
        slope_x = weights[0] - weights[1]
        slope_y = weights[2] - weights[3]
        press_x = 0.01 * (acc_x + 0.5 * slope_x)
        press_y = 0.01 * (acc_y + 0.5 * slope_y)
        acc_x = acc_x + slope_x
        acc_y = acc_y + slope_y
        ue, uw = around[0][0], around[0][1]
        vn, vs = around[1][2], around[1][3]
        extra = [rot * q[1] - press_x, -rot * q[0] - press_y, 0.0, 0.0]
        growth = []
        for c in range(4):
            e, w, n, s = around[c]
            advect = 0.5 * ((ue * e - uw * w) + (vn * n - vs * s))
            growth.append(jnp.where(wet, extra[c] - smooth[c] - advect, 0.0))
        force_u = force_u + d * growth[0]
        force_v = force_v + d * growth[1]
        e_now = jnp.where(
            jnp.logical_and(wet, wet_next), mix[k] / (0.5 * (d + d_next)), 0.0
        )
        inverse = 1.0 / (d + e_up + e_now - e_up * ratio)
        ratio = e_now * inverse
        ratio_buf[k] = ratio
        new_values = []
        for c in range(4):
            val = (d * (q[c] + 0.1 * growth[c]) + e_up * values[c]) * inverse
            val_buf[c, k] = val
            new_values.append(val)
        return acc_x, acc_y, force_u, force_v, e_now, ratio, tuple(new_values)

    zero = jnp.zeros((8, 128), F32)
    carry = (zero, zero, zero, zero, zero, zero, (zero, zero, zero, zero))

    def block_body(n, carry):
        g = n // per_group
        back = lax.rem(128 - 4 * BLOCK * (n - per_group * g), 128)
        rims = (
            [pltpu.roll(bq[c, g], back, 1) for c in range(4)],
            [pltpu.roll(bl[c, g], back, 1) for c in range(4)],
            [pltpu.roll(bcorn[c, g], back, 1) for c in range(2)],
        )
        pl.when(has_s)(lambda: to_north(n).wait_recv())
        pl.when(has_n)(lambda: to_south(n).wait_recv())
        for i in range(BLOCK):
            carry = level(n, i, rims, carry)
        return carry

    carry = lax.fori_loop(0, blocks, block_body, carry)

    for c in waits1:
        c.wait_recv()
    hand, handed = [], []
    for chip in range(chips):
        i = nxt()
        mate = dev(gx, tile_of(my_chip, 1 - core))
        have, want = tile_of(chip, core), tile_of(chip, 1 - core)
        hand.append(rc(all1.at[have], all1.at[have], i, mate))
        handed.append(rc(all1.at[want], all1.at[want], i, mate))
    scale = land_f / safe
    push1[0] = carry[2] * scale
    push1[1] = carry[3] * scale
    push_copies = pair(push1, p2recv)
    for c in push_copies:
        c.start()
    for c in hand:
        c.start()

    def back_body(n, state):
        after, mean_u, mean_v = state
        for i in range(BLOCK):
            k = levels - 1 - n * BLOCK - i
            ratio = ratio_buf[k]
            now = [val_buf[c, k] + ratio * after[c] for c in range(4)]
            val_buf[0, k] = now[0]
            val_buf[1, k] = now[1]
            trc_out[0, k] = now[2]
            trc_out[1, k] = now[3]
            part = jnp.where(k.astype(F32) < be, dz[k], 0.0)
            mean_u = mean_u + part * now[0]
            mean_v = mean_v + part * now[1]
            after = tuple(now)
        return after, mean_u, mean_v

    half = blocks // 3
    solved = lax.fori_loop(0, half, back_body, ((zero,) * 4, zero, zero))
    for c in push_copies:
        c.wait_recv()
    for f in range(2):
        wide2[2 * f] = push1[f]
        wide2[2 * f + 1] = jnp.where(lane < 64, p2recv[1, f], p2recv[0, f])
    starts2, waits2 = peers(wide2, all2)
    for c in starts2:
        c.start()
    all2[t] = wide2[...]
    unused, mean_u, mean_v = lax.fori_loop(half, blocks, back_body, solved)

    count = 8 * tiles
    shape = (count, 128)
    lanes = lax.broadcasted_iota(jnp.int32, shape, 1)
    at_first, at_last = lanes == 0, lanes == 127
    for c in handed:
        c.wait_recv()
    body = pl.ds(8, count)
    above, below = pl.ds(9, count), pl.ds(7, count)
    for ref in (high, flow):
        for h in range(2):
            ref[h, 0:8, :] = jnp.zeros((8, 128), F32)
            ref[h, count + 8:count + 16, :] = jnp.zeros((8, 128), F32)
    for c in waits2:
        c.wait_recv()
    for tile in range(tiles):
        at = slice(8 * tile, 8 * tile + 8)
        f = all1[tile, 8]
        for h in range(2):
            depth = all1[tile, 6 + h]
            sea = jnp.where(depth > 0.0, 1.0, 0.0)
            state[0, h, at] = all1[tile, h]
            state[1, h, at] = all1[tile, 2 + h]
            state[2, h, at] = all1[tile, 4 + h]
            fixed[0, h, at] = sea
            fixed[1, h, at] = 0.05 * depth
            fixed[2, h, at] = 0.1 * f * sea
            fixed[3, h, at] = 0.1 * all2[tile, h] * sea
            fixed[4, h, at] = 0.1 * all2[tile, 2 + h] * sea
    mine = rows_of(t)

    def diff_x(a):
        e = [pltpu.roll(x, 127, 1) for x in a]
        w = [pltpu.roll(x, 1, 1) for x in a]
        return [
            jnp.where(at_last, e[1 - h], e[h]) - jnp.where(at_first, w[1 - h], w[h])
            for h in range(2)
        ]

    def sub_body(i, sums):
        u = [state[1, h] for h in range(2)]
        v = [state[2, h] for h in range(2)]
        for h in range(2):
            flow[h, body] = fixed[1, h] * v[h]
        dx = diff_x([fixed[1, h] * u[h] for h in range(2)])
        tall = []
        for h in range(2):
            dy = flow[h, above] - flow[h, below]
            tall.append((state[0, h] - (dx[h] + dy)) * fixed[0, h])
            high[h, body] = tall[h]
            state[0, h] = tall[h]
        dx = diff_x(tall)
        for h in range(2):
            sea, f = fixed[0, h], fixed[2, h]
            g = 1.25 * sea
            state[1, h] = u[h] * sea + fixed[3, h] + f * v[h] - g * dx[h]
            state[2, h] = v[h] * sea + fixed[4, h] - f * u[h] - g * (high[h, above] - high[h, below])
        return sums[0] + state[1, 0, mine], sums[1] + state[2, 0, mine]

    sum_u, sum_v = lax.fori_loop(0, NSUB, sub_body, (zero, zero))
    surf_out[...] = state[0, 0, mine]
    baro_out[0] = state[1, 0, mine]
    baro_out[1] = state[2, 0, mine]
    shift_u = sum_u * (1.0 / NSUB) - mean_u / safe
    shift_v = sum_v * (1.0 / NSUB) - mean_v / safe

    def out_body(n, carry):
        for i in range(BLOCK):
            k = n * BLOCK + i
            wet = k.astype(F32) < be
            vel_out[0, k] = jnp.where(wet, val_buf[0, k] + shift_u, 0.0)
            vel_out[1, k] = jnp.where(wet, val_buf[1, k] + shift_v, 0.0)
        return carry

    lax.fori_loop(0, blocks, out_body, 0)

    for c in two_d + x_copies + starts1 + hand + push_copies + starts2:
        c.wait_send()
    norths = diag_n + [be_up] + [to_north(n) for n in range(blocks)]
    souths = diag_s + [be_down] + [to_south(n) for n in range(blocks)]
    for c in norths:
        pl.when(has_n)(c.wait_send)
    for c in souths:
        pl.when(has_s)(c.wait_send)


def settle(vel_in, trc_in, surf_in, baro_in, vel_out, trc_out, surf_out, baro_out,
           vel, trc, surf, baro, in_sem, out_sem):
    levels = vel_in.shape[1]
    half = levels // 2
    trips = []
    for src, mid, dst in ((vel_in, vel, vel_out), (trc_in, trc, trc_out)):
        for c in range(2):
            for at in (pl.ds(0, half), pl.ds(half, levels - half)):
                trips.append((src.at[c, at], mid.at[c, at], dst.at[c, at]))
    trips.append((surf_in, surf, surf_out))
    trips.append((baro_in, baro, baro_out))
    ins = [pltpu.make_async_copy(s, m, in_sem.at[i]) for i, (s, m, d) in enumerate(trips)]
    outs = [pltpu.make_async_copy(m, d, out_sem.at[i]) for i, (s, m, d) in enumerate(trips)]
    for c in ins:
        c.start()
    for c, o in zip(ins, outs):
        c.wait()
        o.start()
    for o in outs:
        o.wait()


def shards(nx, ngy, nga, velocity, tracers, mixing, thickness, coriolis, land, bottom, surface, barotropic):
    levels = thickness.shape[0]
    tiles = ngy * nga
    groups = (levels + 31) // 32
    copies = 4 + 2 * (levels // BLOCK) + 2 + 4 + (tiles - 1) + 2 + (tiles - 1)
    tile = (8, 128)
    scratch = [
        (levels,) + tile, (levels,) + tile, (levels,) + tile, (levels,) + tile,
        (6, groups) + tile, (2, 4, groups) + tile, (2, groups) + tile, (2, groups) + tile,
        (4, groups) + tile, (4, groups) + tile, (2, groups) + tile,
        (5,) + tile, (2, 5) + tile, (9,) + tile, (tiles, 9) + tile,
        (2,) + tile, (2, 2) + tile, (4,) + tile, (tiles, 4) + tile,
        (levels,) + tile, (4, levels) + tile, tile, tile,
        (3, 2, 8 * tiles, 128), (5, 2, 8 * tiles, 128), (2, 8 * tiles + 16, 128), (2, 8 * tiles + 16, 128),
    ]
    staged = [
        pltpu.VMEM(velocity.shape, F32), pltpu.VMEM(tracers.shape, F32), pltpu.VMEM(mixing.shape, F32),
        pltpu.SMEM(thickness.shape, F32), pltpu.SMEM(coriolis.shape, F32),
        pltpu.VMEM(land.shape, jnp.int32), pltpu.VMEM(bottom.shape, jnp.int32),
        pltpu.VMEM(surface.shape, F32), pltpu.VMEM(barotropic.shape, F32),
    ]
    vmem = pl.BlockSpec(memory_space=pltpu.VMEM)
    far = pl.BlockSpec(memory_space=pltpu.HBM)
    results = pl.pallas_call(
        functools.partial(kernel, nx, ngy, nga, levels),
        out_shape=(
            jax.ShapeDtypeStruct(velocity.shape, F32),
            jax.ShapeDtypeStruct(tracers.shape, F32),
            jax.ShapeDtypeStruct(surface.shape, F32),
            jax.ShapeDtypeStruct(barotropic.shape, F32),
        ),
        in_specs=[far] * 9,
        out_specs=(vmem, vmem, vmem, vmem),
        scratch_shapes=[pltpu.VMEM(s, F32) for s in scratch]
        + staged
        + [pltpu.SemaphoreType.DMA((copies,)), pltpu.SemaphoreType.DMA((copies,)), pltpu.SemaphoreType.DMA((9,))],
        compiler_params=pltpu.CompilerParams(
            collective_id=0, has_side_effects=True, vmem_limit_bytes=64 * 1024 * 1024
        ),
    )(velocity, tracers, mixing, thickness, coriolis, land, bottom, surface, barotropic)
    anywhere = pl.BlockSpec(memory_space=pltpu.HBM)
    return pl.pallas_call(
        settle,
        out_shape=tuple(jax.ShapeDtypeStruct(r.shape, r.dtype) for r in results),
        in_specs=[anywhere] * 4,
        out_specs=(anywhere,) * 4,
        scratch_shapes=[pltpu.VMEM(r.shape, F32) for r in results]
        + [pltpu.SemaphoreType.DMA((10,)), pltpu.SemaphoreType.DMA((10,))],
        compiler_params=pltpu.CompilerParams(vmem_limit_bytes=64 * 1024 * 1024),
    )(*results)


def solution(mesh):
    sizes = mesh.shape
    return jax.shard_map(
        functools.partial(shards, sizes["gx"], sizes["gy"], sizes["ga"]),
        mesh=mesh,
        in_specs=(
            P(None, None, ("gy", "ga"), "gx"),
            P(None, None, ("gy", "ga"), "gx"),
            P(None, ("gy", "ga"), "gx"),
            P(),
            P(("gy", "ga")),
            P(("gy", "ga"), "gx"),
            P(("gy", "ga"), "gx"),
            P(("gy", "ga"), "gx"),
            P(None, ("gy", "ga"), "gx"),
        ),
        out_specs=(
            P(None, None, ("gy", "ga"), "gx"),
            P(None, None, ("gy", "ga"), "gx"),
            P(("gy", "ga"), "gx"),
            P(None, ("gy", "ga"), "gx"),
        ),
        check_vma=False,
    )
```

```python
import functools
import jax
import jax.numpy as jnp
from jax import lax
from jax.experimental import pallas as pl
from jax.experimental.pallas import tpu as pltpu
from jax.sharding import PartitionSpec as P

NSUB = 30
F32 = jnp.float32
MESH = pl.DeviceIdType.MESH
BLOCK = 8


def kernel(
    nx, ngy, nga, levels,
    vel_in, trc_in, mix_in, dz_in, cor_in, land_in, bot_in, surf_in, baro_in,
    solved_out, small_out,
    ynorth, ysouth, hnorth, hsouth,
    xpack, xrecv, crn, crs, bq, bl, bcorn,
    tile2, t2recv, wide1, all1, push1, p2recv, wide2, all2,
    ratio_buf, val_buf, be_above, be_below, state, fixed, high, flow,
    vel, trc, mix, dz, cor, land, bot, surf, baro,
    send_sem, recv_sem, load_sem,
):
    tiles = ngy * nga
    groups = xpack.shape[1]
    blocks = levels // BLOCK
    per_group = 32 // BLOCK
    loads = [
        pltpu.make_async_copy(src, dst, load_sem.at[i])
        for i, (src, dst) in enumerate([
            (dz_in, dz), (cor_in, cor), (land_in, land), (bot_in, bot), (surf_in, surf),
            (baro_in, baro),
        ] + [
            (src.at[c, pl.ds(at, levels // 2)], dst.at[c, pl.ds(at, levels // 2)])
            for at in (0, levels // 2)
            for src, dst in ((vel_in, vel), (trc_in, trc))
            for c in range(2)
        ] + [(mix_in, mix)])
    ]
    count_loads = len(loads)
    for c in loads:
        c.start()
    gx = lax.axis_index("gx")
    t = lax.axis_index("gy") * nga + lax.axis_index("ga")
    left = lax.rem(gx + nx - 1, nx)
    right = lax.rem(gx + 1, nx)
    has_n = t < tiles - 1
    has_s = t > 0

    def dev(x, tile):
        return {"gx": x, "gy": tile // nga, "ga": lax.rem(tile, nga)}

    up = jnp.minimum(t + 1, tiles - 1)
    down = jnp.maximum(t - 1, 0)

    barrier = pltpu.get_barrier_semaphore()

    def greet(d):
        pl.semaphore_signal(barrier, inc=1, device_id=d, device_id_type=MESH)

    greet(dev(left, t))
    greet(dev(right, t))
    for p in range(1, tiles):
        greet(dev(gx, lax.rem(t + p, tiles)))

    @pl.when(has_n)
    def _():
        greet(dev(left, up))
        greet(dev(right, up))

    @pl.when(has_s)
    def _():
        greet(dev(left, down))
        greet(dev(right, down))

    row = lax.broadcasted_iota(jnp.int32, (8, 128), 0)
    lane = lax.broadcasted_iota(jnp.int32, (8, 128), 1)
    slot = lane // 4
    l4 = lane - 4 * slot
    first_l, last_l = lane == 0, lane == 127
    first_r, last_r = row == 0, row == 7

    for c in loads[:6]:
        c.wait()
    land_i = land[...]
    be = jnp.where(land_i > 0, bot[...], -1).astype(F32)
    land_f = land_i.astype(F32)

    def depth_body(n, acc):
        total, depth = acc
        for i in range(BLOCK):
            k = n * BLOCK + i
            d = dz[k]
            total = total + d
            depth = depth + jnp.where(k.astype(F32) < be, d, 0.0)
        return total, depth

    dz_total, depth_sum = lax.fori_loop(
        0, blocks, depth_body, (jnp.float32(0.0), jnp.zeros((8, 128), F32))
    )
    safe = jnp.maximum(depth_sum, 1.0)
    rot = jnp.zeros((8, 128), F32)
    for r in range(8):
        rot = jnp.where(row == r, cor[r], rot)
    tile2[0] = surf[...]
    tile2[1] = baro[0]
    tile2[2] = baro[1]
    tile2[3] = depth_sum / jnp.broadcast_to(dz_total, (8, 128))
    tile2[4] = be

    pl.semaphore_wait(
        barrier, 2 + tiles - 1 + jnp.where(has_n, 2, 0) + jnp.where(has_s, 2, 0)
    )

    def rc(src, dst, i, d):
        return pltpu.make_async_remote_copy(
            src_ref=src, dst_ref=dst, send_sem=send_sem.at[i], recv_sem=recv_sem.at[i],
            device_id=d, device_id_type=MESH,
        )

    index = [0]

    def nxt():
        index[0] += 1
        return index[0] - 1

    def rows_of(tile):
        return pl.ds(pl.multiple_of(tile * 8, 8), 8)

    def pair(src, recv):
        return [
            rc(src, recv.at[0], nxt(), dev(right, t)),
            rc(src, recv.at[1], nxt(), dev(left, t)),
        ]

    def peers(src, dst):
        starts, waits = [], []
        for p in range(1, tiles):
            i = nxt()
            to = lax.rem(t + p, tiles)
            origin = lax.rem(t + tiles - p, tiles)
            starts.append(rc(src, dst.at[t], i, dev(gx, to)))
            waits.append(rc(src, dst.at[origin], i, dev(gx, to)))
        return starts, waits

    two_d = pair(tile2, t2recv)
    for c in two_d:
        c.start()
    be_up = rc(tile2.at[4], be_below, nxt(), dev(gx, up))
    be_down = rc(tile2.at[4], be_above, nxt(), dev(gx, down))
    pl.when(has_n)(be_up.start)
    pl.when(has_s)(be_down.start)

    @pl.when(jnp.logical_not(has_n))
    def _():
        hnorth[...] = jnp.zeros_like(hnorth)
        crn[...] = jnp.zeros_like(crn)
        be_above[...] = jnp.full_like(be_above, -1.0)

    @pl.when(jnp.logical_not(has_s))
    def _():
        hsouth[...] = jnp.zeros_like(hsouth)
        crs[...] = jnp.zeros_like(crs)
        be_below[...] = jnp.full_like(be_below, -1.0)

    xpack[...] = jnp.zeros_like(xpack)

    def field(c, k):
        return vel[c, k] if c < 2 else trc[c - 2, k]

    def masked(k):
        wet = k.astype(F32) < be
        return [jnp.where(wet, field(c, k), 0.0) for c in range(4)]

    def place(n, first, acc):
        g = n // per_group
        part = n - per_group * g
        here = slot // BLOCK == part
        for j, a in enumerate(acc):
            xpack[first + j, g] = jnp.where(
                here, pltpu.roll(a, 4 * BLOCK * part, 1), xpack[first + j, g]
            )

    def pack_rows(n, carry):
        acc = [jnp.zeros((8, 128), F32)] * 2
        for i in range(BLOCK):
            k = n * BLOCK + i
            q = masked(k)
            ends = [
                jnp.concatenate([a[6:8] for a in q], axis=0),
                jnp.concatenate([a[0:2] for a in q], axis=0),
            ]
            ynorth[k] = ends[0]
            ysouth[k] = ends[1]
            for c in range(2):
                acc[c] = jnp.where(slot == i, pltpu.roll(ends[c], 2 + 4 * i, 1), acc[c])
        place(n, 4, acc)
        pl.when(has_n)(lambda: to_north(n).start())
        pl.when(has_s)(lambda: to_south(n).start())
        return carry

    def pack_columns(n, carry):
        acc = [jnp.zeros((8, 128), F32)] * 4
        for i in range(BLOCK):
            q = masked(n * BLOCK + i)
            for c in range(4):
                acc[c] = jnp.where(slot == i, pltpu.roll(q[c], 2 + 4 * i, 1), acc[c])
        place(n, 0, acc)
        return carry

    first_north, first_south = index[0], index[0] + blocks
    index[0] += 2 * blocks

    def to_north(n):
        span = pl.ds(n * BLOCK, BLOCK)
        return rc(ynorth.at[span], hsouth.at[span], first_north + n, dev(gx, up))

    def to_south(n):
        span = pl.ds(n * BLOCK, BLOCK)
        return rc(ysouth.at[span], hnorth.at[span], first_south + n, dev(gx, down))

    for c in loads[6:10]:
        c.wait()
    lax.fori_loop(0, blocks // 2, pack_rows, 0)
    for c in loads[10:14]:
        c.wait()
    lax.fori_loop(blocks // 2, blocks, pack_rows, 0)
    diag_n = [
        rc(xpack.at[4], crs.at[1], nxt(), dev(left, up)),
        rc(xpack.at[4], crs.at[0], nxt(), dev(right, up)),
    ]
    diag_s = [
        rc(xpack.at[5], crn.at[1], nxt(), dev(left, down)),
        rc(xpack.at[5], crn.at[0], nxt(), dev(right, down)),
    ]
    for c in diag_n:
        pl.when(has_n)(c.start)
    for c in diag_s:
        pl.when(has_s)(c.start)

    lax.fori_loop(0, blocks, pack_columns, 0)
    x_copies = pair(xpack.at[pl.ds(0, 4)], xrecv)
    for c in x_copies:
        c.start()

    for c in two_d:
        c.wait_recv()
    for f in range(4):
        wide1[2 * f] = tile2[f]
        wide1[2 * f + 1] = jnp.where(lane < 64, t2recv[1, f], t2recv[0, f])
    wide1[8] = rot
    all1[t] = wide1[...]
    core = lax.rem(t // nga, 2)
    stride = 2 * nga
    chips = tiles // 2
    my_chip = (t // stride) * nga + lax.rem(t, nga)

    def tile_of(chip, on):
        return (chip // nga) * stride + on * nga + lax.rem(chip, nga)

    starts1, waits1 = [], []
    for p in range(1, chips):
        i = nxt()
        to = dev(gx, tile_of(lax.rem(my_chip + p, chips), core))
        origin = tile_of(lax.rem(my_chip + chips - p, chips), core)
        starts1.append(rc(wide1, all1.at[t], i, to))
        waits1.append(rc(wide1, all1.at[origin], i, to))
    for c in starts1:
        c.start()

    be_side = jnp.where(
        l4 == 1,
        jnp.broadcast_to(t2recv[0, 4][:, 127:128], (8, 128)),
        jnp.broadcast_to(t2recv[1, 4][:, 0:1], (8, 128)),
    )
    for c in x_copies:
        c.wait_recv()
    for c in diag_n:
        pl.when(has_s)(c.wait_recv)
    for c in diag_s:
        pl.when(has_n)(c.wait_recv)

    def close(a):
        return jnp.where(l4 == 1, a, pltpu.roll(a, 126, 1))

    low = l4 < 2
    for g in range(groups):
        corner_n = jnp.where(low, crn[0, g], crn[1, g])
        corner_s = jnp.where(low, crs[0, g], crs[1, g])
        bcorn[0, g] = close(corner_n)
        bcorn[1, g] = close(corner_s)
        wet = (32 * g + slot).astype(F32) < be_side
        for c in range(4):
            a = jnp.where(low, xrecv[0, c, g], xrecv[1, c, g])
            mine = xpack[c, g]
            sides = jnp.where(
                l4 == 1,
                pltpu.roll(a, 1, 1) + pltpu.roll(mine, 127, 1),
                pltpu.roll(a, 127, 1) + pltpu.roll(mine, 1, 1),
            )
            north = jnp.where(
                last_r, jnp.broadcast_to(corner_n[2 * c:2 * c + 1], (8, 128)), pltpu.roll(a, 7, 0)
            )
            south = jnp.where(
                first_r, jnp.broadcast_to(corner_s[2 * c + 1:2 * c + 2], (8, 128)), pltpu.roll(a, 1, 0)
            )
            lap = jnp.where(wet, sides + north + south - 4.0 * a, 0.0)
            bq[c, g] = close(a)
            bl[c, g] = close(lap)

    pl.when(has_s)(be_up.wait_recv)
    pl.when(has_n)(be_down.wait_recv)
    loads[14].wait()
    be_n = jnp.broadcast_to(be_above[0:1, :], (8, 128))
    be_s = jnp.broadcast_to(be_below[7:8, :], (8, 128))

    def east_west(a, h):
        return (
            jnp.where(last_l, h, pltpu.roll(a, 127, 1)),
            jnp.where(first_l, h, pltpu.roll(a, 1, 1)),
        )

    def row_of(a, r):
        return jnp.broadcast_to(a[r:r + 1], (8, 128))

    def level(n, i, rims, carry):
        rim_q, rim_l, rim_c = rims
        k = n * BLOCK + i
        acc_x, acc_y, force_u, force_v, e_up, ratio, values = carry
        kf = k.astype(F32)
        d = dz[k]
        k_next = jnp.minimum(k + 1, levels - 1)
        d_next = dz[k_next]
        turn = 127 - 4 * i
        wet = kf < be
        wet_next = jnp.logical_and(kf + 1.0 < be, k + 1 < levels)
        q = [jnp.where(wet, field(c, k), 0.0) for c in range(4)]
        hn, hs = hnorth[k], hsouth[k]
        he, hw = east_west(hn, pltpu.roll(rim_c[0], turn, 1))
        lap_n = jnp.where(
            kf < be_n, pltpu.roll(hn + ynorth[k], 7, 0) + he + hw - 4.0 * hn, 0.0
        )
        he, hw = east_west(hs, pltpu.roll(rim_c[1], turn, 1))
        lap_s = jnp.where(
            kf < be_s, pltpu.roll(hs + ysouth[k], 1, 0) + he + hw - 4.0 * hs, 0.0
        )
        around, smooth = [], []
        for c in range(4):
            a = q[c]
            e, w = east_west(a, pltpu.roll(rim_q[c], turn, 1))
            n = jnp.where(last_r, jnp.broadcast_to(hnorth[k, 2 * c:2 * c + 1, :], (8, 128)), pltpu.roll(a, 7, 0))
            s = jnp.where(first_r, jnp.broadcast_to(hsouth[k, 2 * c + 1:2 * c + 2, :], (8, 128)), pltpu.roll(a, 1, 0))
            around.append((e, w, n, s))
            lap = jnp.where(wet, (e + w) + (n + s) - 4.0 * a, 0.0)
            e, w = east_west(lap, pltpu.roll(rim_l[c], turn, 1))
            n = jnp.where(last_r, row_of(lap_n, 2 * c), pltpu.roll(lap, 7, 0))
            s = jnp.where(first_r, row_of(lap_s, 2 * c + 1), pltpu.roll(lap, 1, 0))
            smooth.append(0.02 * ((e + w) + (n + s) - 4.0 * lap))
        weights = [
            (0.1 * around[3][i] - 0.2 * around[2][i]) * d for i in range(4)
        ]
        slope_x = weights[0] - weights[1]
        slope_y = weights[2] - weights[3]
        press_x = 0.01 * (acc_x + 0.5 * slope_x)
        press_y = 0.01 * (acc_y + 0.5 * slope_y)
        acc_x = acc_x + slope_x
        acc_y = acc_y + slope_y
        ue, uw = around[0][0], around[0][1]
        vn, vs = around[1][2], around[1][3]
        extra = [rot * q[1] - press_x, -rot * q[0] - press_y, 0.0, 0.0]
        growth = []
        for c in range(4):
            e, w, n, s = around[c]
            advect = 0.5 * ((ue * e - uw * w) + (vn * n - vs * s))
            growth.append(jnp.where(wet, extra[c] - smooth[c] - advect, 0.0))
        force_u = force_u + d * growth[0]
        force_v = force_v + d * growth[1]
        e_now = jnp.where(
            jnp.logical_and(wet, wet_next), mix[k] / (0.5 * (d + d_next)), 0.0
        )
        inverse = 1.0 / (d + e_up + e_now - e_up * ratio)
        ratio = e_now * inverse
        ratio_buf[k] = ratio
        new_values = []
        for c in range(4):
            val = (d * (q[c] + 0.1 * growth[c]) + e_up * values[c]) * inverse
            val_buf[c, k] = val
            new_values.append(val)
        return acc_x, acc_y, force_u, force_v, e_now, ratio, tuple(new_values)

    zero = jnp.zeros((8, 128), F32)
    carry = (zero, zero, zero, zero, zero, zero, (zero, zero, zero, zero))

    def block_body(n, carry):
        g = n // per_group
        back = lax.rem(128 - 4 * BLOCK * (n - per_group * g), 128)
        rims = (
            [pltpu.roll(bq[c, g], back, 1) for c in range(4)],
            [pltpu.roll(bl[c, g], back, 1) for c in range(4)],
            [pltpu.roll(bcorn[c, g], back, 1) for c in range(2)],
        )
        pl.when(has_s)(lambda: to_north(n).wait_recv())
        pl.when(has_n)(lambda: to_south(n).wait_recv())
        for i in range(BLOCK):
            carry = level(n, i, rims, carry)
        return carry

    carry = lax.fori_loop(0, blocks, block_body, carry)

    for c in waits1:
        c.wait_recv()
    hand, handed = [], []
    for chip in range(chips):
        i = nxt()
        mate = dev(gx, tile_of(my_chip, 1 - core))
        have, want = tile_of(chip, core), tile_of(chip, 1 - core)
        hand.append(rc(all1.at[have], all1.at[have], i, mate))
        handed.append(rc(all1.at[want], all1.at[want], i, mate))
    scale = land_f / safe
    push1[0] = carry[2] * scale
    push1[1] = carry[3] * scale
    push_copies = pair(push1, p2recv)
    for c in push_copies:
        c.start()
    for c in hand:
        c.start()

    def back_body(n, state):
        after, mean_u, mean_v = state
        for i in range(BLOCK):
            k = levels - 1 - n * BLOCK - i
            ratio = ratio_buf[k]
            now = [val_buf[c, k] + ratio * after[c] for c in range(4)]
            val_buf[0, k] = now[0]
            val_buf[1, k] = now[1]
            val_buf[2, k] = now[2]
            val_buf[3, k] = now[3]
            part = jnp.where(k.astype(F32) < be, dz[k], 0.0)
            mean_u = mean_u + part * now[0]
            mean_v = mean_v + part * now[1]
            after = tuple(now)
        return after, mean_u, mean_v

    half = blocks // 3
    solved = lax.fori_loop(0, half, back_body, ((zero,) * 4, zero, zero))
    for c in push_copies:
        c.wait_recv()
    for f in range(2):
        wide2[2 * f] = push1[f]
        wide2[2 * f + 1] = jnp.where(lane < 64, p2recv[1, f], p2recv[0, f])
    starts2, waits2 = peers(wide2, all2)
    for c in starts2:
        c.start()
    all2[t] = wide2[...]
    unused, mean_u, mean_v = lax.fori_loop(half, blocks, back_body, solved)
    leaving = [
        pltpu.make_async_copy(val_buf.at[c], solved_out.at[c], load_sem.at[count_loads + c])
        for c in range(4)
    ]
    for c in leaving:
        c.start()

    count = 8 * tiles
    shape = (count, 128)
    lanes = lax.broadcasted_iota(jnp.int32, shape, 1)
    at_first, at_last = lanes == 0, lanes == 127
    for c in handed:
        c.wait_recv()
    body = pl.ds(8, count)
    above, below = pl.ds(9, count), pl.ds(7, count)
    for ref in (high, flow):
        for h in range(2):
            ref[h, 0:8, :] = jnp.zeros((8, 128), F32)
            ref[h, count + 8:count + 16, :] = jnp.zeros((8, 128), F32)
    for c in waits2:
        c.wait_recv()
    for tile in range(tiles):
        at = slice(8 * tile, 8 * tile + 8)
        f = all1[tile, 8]
        for h in range(2):
            depth = all1[tile, 6 + h]
            sea = jnp.where(depth > 0.0, 1.0, 0.0)
            state[0, h, at] = all1[tile, h]
            state[1, h, at] = all1[tile, 2 + h]
            state[2, h, at] = all1[tile, 4 + h]
            fixed[0, h, at] = sea
            fixed[1, h, at] = 0.05 * depth
            fixed[2, h, at] = 0.1 * f * sea
            fixed[3, h, at] = 0.1 * all2[tile, h] * sea
            fixed[4, h, at] = 0.1 * all2[tile, 2 + h] * sea
    mine = rows_of(t)

    def diff_x(a):
        e = [pltpu.roll(x, 127, 1) for x in a]
        w = [pltpu.roll(x, 1, 1) for x in a]
        return [
            jnp.where(at_last, e[1 - h], e[h]) - jnp.where(at_first, w[1 - h], w[h])
            for h in range(2)
        ]

    def sub_body(i, sums):
        u = [state[1, h] for h in range(2)]
        v = [state[2, h] for h in range(2)]
        for h in range(2):
            flow[h, body] = fixed[1, h] * v[h]
        dx = diff_x([fixed[1, h] * u[h] for h in range(2)])
        tall = []
        for h in range(2):
            dy = flow[h, above] - flow[h, below]
            tall.append((state[0, h] - (dx[h] + dy)) * fixed[0, h])
            high[h, body] = tall[h]
            state[0, h] = tall[h]
        dx = diff_x(tall)
        for h in range(2):
            sea, f = fixed[0, h], fixed[2, h]
            g = 1.25 * sea
            state[1, h] = u[h] * sea + fixed[3, h] + f * v[h] - g * dx[h]
            state[2, h] = v[h] * sea + fixed[4, h] - f * u[h] - g * (high[h, above] - high[h, below])
        return sums[0] + state[1, 0, mine], sums[1] + state[2, 0, mine]

    sum_u, sum_v = lax.fori_loop(0, NSUB, sub_body, (zero, zero))
    small_out[0] = state[0, 0, mine]
    small_out[1] = state[1, 0, mine]
    small_out[2] = state[2, 0, mine]
    small_out[3] = sum_u * (1.0 / NSUB) - mean_u / safe
    small_out[4] = sum_v * (1.0 / NSUB) - mean_v / safe
    small_out[5] = be

    for c in leaving:
        c.wait()
    for c in two_d + x_copies + starts1 + hand + push_copies + starts2:
        c.wait_send()
    norths = diag_n + [be_up] + [to_north(n) for n in range(blocks)]
    souths = diag_s + [be_down] + [to_south(n) for n in range(blocks)]
    for c in norths:
        pl.when(has_n)(c.wait_send)
    for c in souths:
        pl.when(has_s)(c.wait_send)


def settle(solved_in, small_in, vel_out, trc_out, surf_out, baro_out,
           solved, small, in_sem, out_sem):
    levels = solved_in.shape[1]
    half = levels // 2
    first = pltpu.make_async_copy(small_in, small, in_sem.at[0])
    first.start()
    trips = []
    for c in range(4):
        dst = vel_out if c < 2 else trc_out
        for at in (0, half):
            span = pl.ds(at, half)
            trips.append((c, at, solved_in.at[c, span], solved.at[c, span], dst.at[c % 2, span]))
    ins = [pltpu.make_async_copy(x[2], x[3], in_sem.at[1 + i]) for i, x in enumerate(trips)]
    outs = [pltpu.make_async_copy(x[3], x[4], out_sem.at[2 + i]) for i, x in enumerate(trips)]
    ends = [
        pltpu.make_async_copy(small.at[0], surf_out, out_sem.at[0]),
        pltpu.make_async_copy(small.at[pl.ds(1, 2)], baro_out, out_sem.at[1]),
    ]
    for c in ins:
        c.start()
    first.wait()
    for c in ends:
        c.start()
    be = small[5]
    for i, (c, at, *unused) in enumerate(trips):
        ins[i].wait()
        if c < 2:
            shift = small[3 + c]

            def body(n, carry):
                for j in range(BLOCK):
                    k = at + n * BLOCK + j
                    wet = k.astype(F32) < be
                    solved[c, k] = jnp.where(wet, solved[c, k] + shift, 0.0)
                return carry

            lax.fori_loop(0, half // BLOCK, body, 0)
        outs[i].start()
    for c in ends + outs:
        c.wait()


def shards(nx, ngy, nga, velocity, tracers, mixing, thickness, coriolis, land, bottom, surface, barotropic):
    levels = thickness.shape[0]
    tiles = ngy * nga
    groups = (levels + 31) // 32
    copies = 4 + 2 * (levels // BLOCK) + 2 + 4 + (tiles - 1) + 2 + (tiles - 1)
    tile = (8, 128)
    scratch = [
        (levels,) + tile, (levels,) + tile, (levels,) + tile, (levels,) + tile,
        (6, groups) + tile, (2, 4, groups) + tile, (2, groups) + tile, (2, groups) + tile,
        (4, groups) + tile, (4, groups) + tile, (2, groups) + tile,
        (5,) + tile, (2, 5) + tile, (9,) + tile, (tiles, 9) + tile,
        (2,) + tile, (2, 2) + tile, (4,) + tile, (tiles, 4) + tile,
        (levels,) + tile, (4, levels) + tile, tile, tile,
        (3, 2, 8 * tiles, 128), (5, 2, 8 * tiles, 128), (2, 8 * tiles + 16, 128), (2, 8 * tiles + 16, 128),
    ]
    staged = [
        pltpu.VMEM(velocity.shape, F32), pltpu.VMEM(tracers.shape, F32), pltpu.VMEM(mixing.shape, F32),
        pltpu.SMEM(thickness.shape, F32), pltpu.SMEM(coriolis.shape, F32),
        pltpu.VMEM(land.shape, jnp.int32), pltpu.VMEM(bottom.shape, jnp.int32),
        pltpu.VMEM(surface.shape, F32), pltpu.VMEM(barotropic.shape, F32),
    ]
    vmem = pl.BlockSpec(memory_space=pltpu.VMEM)
    far = pl.BlockSpec(memory_space=pltpu.HBM)
    results = pl.pallas_call(
        functools.partial(kernel, nx, ngy, nga, levels),
        out_shape=(
            jax.ShapeDtypeStruct((4, levels) + tile, F32),
            jax.ShapeDtypeStruct((6,) + tile, F32),
        ),
        in_specs=[far] * 9,
        out_specs=(far, vmem),
        scratch_shapes=[pltpu.VMEM(s, F32) for s in scratch]
        + staged
        + [pltpu.SemaphoreType.DMA((copies,)), pltpu.SemaphoreType.DMA((copies,)), pltpu.SemaphoreType.DMA((19,))],
        compiler_params=pltpu.CompilerParams(
            collective_id=0, has_side_effects=True, vmem_limit_bytes=64 * 1024 * 1024
        ),
    )(velocity, tracers, mixing, thickness, coriolis, land, bottom, surface, barotropic)
    anywhere = pl.BlockSpec(memory_space=pltpu.HBM)
    return pl.pallas_call(
        settle,
        out_shape=tuple(
            jax.ShapeDtypeStruct(r.shape, F32) for r in (velocity, tracers, surface, barotropic)
        ),
        in_specs=[anywhere] * 2,
        out_specs=(anywhere,) * 4,
        scratch_shapes=[pltpu.VMEM(r.shape, F32) for r in results]
        + [pltpu.SemaphoreType.DMA((10,)), pltpu.SemaphoreType.DMA((10,))],
        compiler_params=pltpu.CompilerParams(vmem_limit_bytes=64 * 1024 * 1024),
    )(*results)


def solution(mesh):
    sizes = mesh.shape
    return jax.shard_map(
        functools.partial(shards, sizes["gx"], sizes["gy"], sizes["ga"]),
        mesh=mesh,
        in_specs=(
            P(None, None, ("gy", "ga"), "gx"),
            P(None, None, ("gy", "ga"), "gx"),
            P(None, ("gy", "ga"), "gx"),
            P(),
            P(("gy", "ga")),
            P(("gy", "ga"), "gx"),
            P(("gy", "ga"), "gx"),
            P(("gy", "ga"), "gx"),
            P(None, ("gy", "ga"), "gx"),
        ),
        out_specs=(
            P(None, None, ("gy", "ga"), "gx"),
            P(None, None, ("gy", "ga"), "gx"),
            P(("gy", "ga"), "gx"),
            P(None, ("gy", "ga"), "gx"),
        ),
        check_vma=False,
    )
```

```python
import functools
import jax
import jax.numpy as jnp
from jax import lax
from jax.experimental import pallas as pl
from jax.experimental.pallas import tpu as pltpu
from jax.sharding import PartitionSpec as P

NSUB = 30
F32 = jnp.float32
MESH = pl.DeviceIdType.MESH
BLOCK = 8


def kernel(
    nx, ngy, nga, levels,
    vel_in, trc_in, mix_in, dz_in, cor_in, land_in, bot_in, surf_in, baro_in,
    solved_out, small_out,
    ynorth, ysouth, hnorth, hsouth,
    xpack, xrecv, crn, crs, bq, bl, bcorn,
    tile2, t2recv, wide1, all1, push1, p2recv, wide2, all2,
    ratio_buf, val_buf, be_above, be_below, state, fixed, high, flow,
    vel, trc, mix, dz, cor, land, bot, surf, baro,
    send_sem, recv_sem, load_sem,
):
    tiles = ngy * nga
    groups = xpack.shape[1]
    blocks = levels // BLOCK
    per_group = 32 // BLOCK
    loads = [
        pltpu.make_async_copy(src, dst, load_sem.at[i])
        for i, (src, dst) in enumerate([
            (dz_in, dz), (cor_in, cor), (land_in, land), (bot_in, bot), (surf_in, surf),
            (baro_in, baro),
        ] + [
            (src.at[c, pl.ds(at, levels // 2)], dst.at[c, pl.ds(at, levels // 2)])
            for at in (0, levels // 2)
            for src, dst in ((vel_in, vel), (trc_in, trc))
            for c in range(2)
        ] + [(mix_in, mix)])
    ]
    count_loads = len(loads)
    for c in loads:
        c.start()
    gx = lax.axis_index("gx")
    t = lax.axis_index("gy") * nga + lax.axis_index("ga")
    left = lax.rem(gx + nx - 1, nx)
    right = lax.rem(gx + 1, nx)
    has_n = t < tiles - 1
    has_s = t > 0

    def dev(x, tile):
        return {"gx": x, "gy": tile // nga, "ga": lax.rem(tile, nga)}

    up = jnp.minimum(t + 1, tiles - 1)
    down = jnp.maximum(t - 1, 0)

    barrier = pltpu.get_barrier_semaphore()

    def greet(d):
        pl.semaphore_signal(barrier, inc=1, device_id=d, device_id_type=MESH)

    greet(dev(left, t))
    greet(dev(right, t))
    for p in range(1, tiles):
        greet(dev(gx, lax.rem(t + p, tiles)))

    @pl.when(has_n)
    def _():
        greet(dev(left, up))
        greet(dev(right, up))

    @pl.when(has_s)
    def _():
        greet(dev(left, down))
        greet(dev(right, down))

    row = lax.broadcasted_iota(jnp.int32, (8, 128), 0)
    lane = lax.broadcasted_iota(jnp.int32, (8, 128), 1)
    slot = lane // 4
    l4 = lane - 4 * slot
    first_l, last_l = lane == 0, lane == 127
    first_r, last_r = row == 0, row == 7

    for c in loads[:6]:
        c.wait()
    land_i = land[...]
    be = jnp.where(land_i > 0, bot[...], -1).astype(F32)
    land_f = land_i.astype(F32)

    def depth_body(n, acc):
        total, depth = acc
        for i in range(BLOCK):
            k = n * BLOCK + i
            d = dz[k]
            total = total + d
            depth = depth + jnp.where(k.astype(F32) < be, d, 0.0)
        return total, depth

    dz_total, depth_sum = lax.fori_loop(
        0, blocks, depth_body, (jnp.float32(0.0), jnp.zeros((8, 128), F32))
    )
    safe = jnp.maximum(depth_sum, 1.0)
    rot = jnp.zeros((8, 128), F32)
    for r in range(8):
        rot = jnp.where(row == r, cor[r], rot)
    tile2[0] = surf[...]
    tile2[1] = baro[0]
    tile2[2] = baro[1]
    tile2[3] = depth_sum / jnp.broadcast_to(dz_total, (8, 128))
    tile2[4] = be

    pl.semaphore_wait(
        barrier, 2 + tiles - 1 + jnp.where(has_n, 2, 0) + jnp.where(has_s, 2, 0)
    )

    def rc(src, dst, i, d):
        return pltpu.make_async_remote_copy(
            src_ref=src, dst_ref=dst, send_sem=send_sem.at[i], recv_sem=recv_sem.at[i],
            device_id=d, device_id_type=MESH,
        )

    index = [0]

    def nxt():
        index[0] += 1
        return index[0] - 1

    def rows_of(tile):
        return pl.ds(pl.multiple_of(tile * 8, 8), 8)

    def pair(src, recv):
        return [
            rc(src, recv.at[0], nxt(), dev(right, t)),
            rc(src, recv.at[1], nxt(), dev(left, t)),
        ]

    def peers(src, dst):
        starts, waits = [], []
        for p in range(1, tiles):
            i = nxt()
            to = lax.rem(t + p, tiles)
            origin = lax.rem(t + tiles - p, tiles)
            starts.append(rc(src, dst.at[t], i, dev(gx, to)))
            waits.append(rc(src, dst.at[origin], i, dev(gx, to)))
        return starts, waits

    two_d = pair(tile2, t2recv)
    for c in two_d:
        c.start()
    be_up = rc(tile2.at[4], be_below, nxt(), dev(gx, up))
    be_down = rc(tile2.at[4], be_above, nxt(), dev(gx, down))
    pl.when(has_n)(be_up.start)
    pl.when(has_s)(be_down.start)

    @pl.when(jnp.logical_not(has_n))
    def _():
        hnorth[...] = jnp.zeros_like(hnorth)
        crn[...] = jnp.zeros_like(crn)
        be_above[...] = jnp.full_like(be_above, -1.0)

    @pl.when(jnp.logical_not(has_s))
    def _():
        hsouth[...] = jnp.zeros_like(hsouth)
        crs[...] = jnp.zeros_like(crs)
        be_below[...] = jnp.full_like(be_below, -1.0)

    xpack[...] = jnp.zeros_like(xpack)

    def field(c, k):
        return vel[c, k] if c < 2 else trc[c - 2, k]

    def masked(k):
        wet = k.astype(F32) < be
        return [jnp.where(wet, field(c, k), 0.0) for c in range(4)]

    def place(n, first, acc):
        g = n // per_group
        part = n - per_group * g
        here = slot // BLOCK == part
        for j, a in enumerate(acc):
            xpack[first + j, g] = jnp.where(
                here, pltpu.roll(a, 4 * BLOCK * part, 1), xpack[first + j, g]
            )

    def pack_rows(n, carry):
        acc = [jnp.zeros((8, 128), F32)] * 2
        for i in range(BLOCK):
            k = n * BLOCK + i
            q = masked(k)
            ends = [
                jnp.concatenate([a[6:8] for a in q], axis=0),
                jnp.concatenate([a[0:2] for a in q], axis=0),
            ]
            ynorth[k] = ends[0]
            ysouth[k] = ends[1]
            for c in range(2):
                acc[c] = jnp.where(slot == i, pltpu.roll(ends[c], 2 + 4 * i, 1), acc[c])
        place(n, 4, acc)
        pl.when(has_n)(lambda: to_north(n).start())
        pl.when(has_s)(lambda: to_south(n).start())
        g = n // per_group
        full = jnp.logical_or(n - per_group * g == per_group - 1, n == blocks - 1)
        pl.when(jnp.logical_and(full, has_n))(lambda: start_all(diag_n(g)))
        pl.when(jnp.logical_and(full, has_s))(lambda: start_all(diag_s(g)))
        return carry

    def pack_columns(n, carry):
        acc = [jnp.zeros((8, 128), F32)] * 4
        for i in range(BLOCK):
            q = masked(n * BLOCK + i)
            for c in range(4):
                acc[c] = jnp.where(slot == i, pltpu.roll(q[c], 2 + 4 * i, 1), acc[c])
        place(n, 0, acc)
        return carry

    first_north, first_south = index[0], index[0] + blocks
    first_diag = index[0] + 2 * blocks
    index[0] += 2 * blocks + 4 * groups

    def diag_n(g):
        i = first_diag + g
        return [
            rc(xpack.at[4, g], crs.at[1, g], i, dev(left, up)),
            rc(xpack.at[4, g], crs.at[0, g], i + groups, dev(right, up)),
        ]

    def diag_s(g):
        i = first_diag + 2 * groups + g
        return [
            rc(xpack.at[5, g], crn.at[1, g], i, dev(left, down)),
            rc(xpack.at[5, g], crn.at[0, g], i + groups, dev(right, down)),
        ]

    def start_all(copies):
        for c in copies:
            c.start()

    def recv_all(copies):
        for c in copies:
            c.wait_recv()

    def to_north(n):
        span = pl.ds(n * BLOCK, BLOCK)
        return rc(ynorth.at[span], hsouth.at[span], first_north + n, dev(gx, up))

    def to_south(n):
        span = pl.ds(n * BLOCK, BLOCK)
        return rc(ysouth.at[span], hnorth.at[span], first_south + n, dev(gx, down))

    for c in loads[6:10]:
        c.wait()
    lax.fori_loop(0, blocks // 2, pack_rows, 0)
    for c in loads[10:14]:
        c.wait()
    lax.fori_loop(blocks // 2, blocks, pack_rows, 0)
    lax.fori_loop(0, blocks, pack_columns, 0)
    x_copies = pair(xpack.at[pl.ds(0, 4)], xrecv)
    for c in x_copies:
        c.start()

    for c in two_d:
        c.wait_recv()
    for f in range(4):
        wide1[2 * f] = tile2[f]
        wide1[2 * f + 1] = jnp.where(lane < 64, t2recv[1, f], t2recv[0, f])
    wide1[8] = rot
    all1[t] = wide1[...]
    core = lax.rem(t // nga, 2)
    stride = 2 * nga
    chips = tiles // 2
    my_chip = (t // stride) * nga + lax.rem(t, nga)

    def tile_of(chip, on):
        return (chip // nga) * stride + on * nga + lax.rem(chip, nga)

    starts1, waits1 = [], []
    for p in range(1, chips):
        i = nxt()
        to = dev(gx, tile_of(lax.rem(my_chip + p, chips), core))
        origin = tile_of(lax.rem(my_chip + chips - p, chips), core)
        starts1.append(rc(wide1, all1.at[t], i, to))
        waits1.append(rc(wide1, all1.at[origin], i, to))
    for c in starts1:
        c.start()

    be_side = jnp.where(
        l4 == 1,
        jnp.broadcast_to(t2recv[0, 4][:, 127:128], (8, 128)),
        jnp.broadcast_to(t2recv[1, 4][:, 0:1], (8, 128)),
    )
    for c in x_copies:
        c.wait_recv()

    def close(a):
        return jnp.where(l4 == 1, a, pltpu.roll(a, 126, 1))

    low = l4 < 2

    def open_group(g):
        pl.when(has_s)(lambda: recv_all(diag_n(g)))
        pl.when(has_n)(lambda: recv_all(diag_s(g)))
        corner_n = jnp.where(low, crn[0, g], crn[1, g])
        corner_s = jnp.where(low, crs[0, g], crs[1, g])
        bcorn[0, g] = close(corner_n)
        bcorn[1, g] = close(corner_s)
        wet = (32 * g + slot).astype(F32) < be_side
        for c in range(4):
            a = jnp.where(low, xrecv[0, c, g], xrecv[1, c, g])
            mine = xpack[c, g]
            sides = jnp.where(
                l4 == 1,
                pltpu.roll(a, 1, 1) + pltpu.roll(mine, 127, 1),
                pltpu.roll(a, 127, 1) + pltpu.roll(mine, 1, 1),
            )
            north = jnp.where(
                last_r, jnp.broadcast_to(corner_n[2 * c:2 * c + 1], (8, 128)), pltpu.roll(a, 7, 0)
            )
            south = jnp.where(
                first_r, jnp.broadcast_to(corner_s[2 * c + 1:2 * c + 2], (8, 128)), pltpu.roll(a, 1, 0)
            )
            lap = jnp.where(wet, sides + north + south - 4.0 * a, 0.0)
            bq[c, g] = close(a)
            bl[c, g] = close(lap)

    pl.when(has_s)(be_up.wait_recv)
    pl.when(has_n)(be_down.wait_recv)
    loads[14].wait()
    be_n = jnp.broadcast_to(be_above[0:1, :], (8, 128))
    be_s = jnp.broadcast_to(be_below[7:8, :], (8, 128))

    def east_west(a, h):
        return (
            jnp.where(last_l, h, pltpu.roll(a, 127, 1)),
            jnp.where(first_l, h, pltpu.roll(a, 1, 1)),
        )

    def row_of(a, r):
        return jnp.broadcast_to(a[r:r + 1], (8, 128))

    def level(n, i, rims, carry):
        rim_q, rim_l, rim_c = rims
        k = n * BLOCK + i
        acc_x, acc_y, force_u, force_v, e_up, ratio, values = carry
        kf = k.astype(F32)
        d = dz[k]
        k_next = jnp.minimum(k + 1, levels - 1)
        d_next = dz[k_next]
        turn = 127 - 4 * i
        wet = kf < be
        wet_next = jnp.logical_and(kf + 1.0 < be, k + 1 < levels)
        q = [jnp.where(wet, field(c, k), 0.0) for c in range(4)]
        hn, hs = hnorth[k], hsouth[k]
        he, hw = east_west(hn, pltpu.roll(rim_c[0], turn, 1))
        lap_n = jnp.where(
            kf < be_n, pltpu.roll(hn + ynorth[k], 7, 0) + he + hw - 4.0 * hn, 0.0
        )
        he, hw = east_west(hs, pltpu.roll(rim_c[1], turn, 1))
        lap_s = jnp.where(
            kf < be_s, pltpu.roll(hs + ysouth[k], 1, 0) + he + hw - 4.0 * hs, 0.0
        )
        around, smooth = [], []
        for c in range(4):
            a = q[c]
            e, w = east_west(a, pltpu.roll(rim_q[c], turn, 1))
            n = jnp.where(last_r, jnp.broadcast_to(hnorth[k, 2 * c:2 * c + 1, :], (8, 128)), pltpu.roll(a, 7, 0))
            s = jnp.where(first_r, jnp.broadcast_to(hsouth[k, 2 * c + 1:2 * c + 2, :], (8, 128)), pltpu.roll(a, 1, 0))
            around.append((e, w, n, s))
            lap = jnp.where(wet, (e + w) + (n + s) - 4.0 * a, 0.0)
            e, w = east_west(lap, pltpu.roll(rim_l[c], turn, 1))
            n = jnp.where(last_r, row_of(lap_n, 2 * c), pltpu.roll(lap, 7, 0))
            s = jnp.where(first_r, row_of(lap_s, 2 * c + 1), pltpu.roll(lap, 1, 0))
            smooth.append(0.02 * ((e + w) + (n + s) - 4.0 * lap))
        weights = [
            (0.1 * around[3][i] - 0.2 * around[2][i]) * d for i in range(4)
        ]
        slope_x = weights[0] - weights[1]
        slope_y = weights[2] - weights[3]
        press_x = 0.01 * (acc_x + 0.5 * slope_x)
        press_y = 0.01 * (acc_y + 0.5 * slope_y)
        acc_x = acc_x + slope_x
        acc_y = acc_y + slope_y
        ue, uw = around[0][0], around[0][1]
        vn, vs = around[1][2], around[1][3]
        extra = [rot * q[1] - press_x, -rot * q[0] - press_y, 0.0, 0.0]
        growth = []
        for c in range(4):
            e, w, n, s = around[c]
            advect = 0.5 * ((ue * e - uw * w) + (vn * n - vs * s))
            growth.append(jnp.where(wet, extra[c] - smooth[c] - advect, 0.0))
        force_u = force_u + d * growth[0]
        force_v = force_v + d * growth[1]
        e_now = jnp.where(
            jnp.logical_and(wet, wet_next), mix[k] / (0.5 * (d + d_next)), 0.0
        )
        inverse = 1.0 / (d + e_up + e_now - e_up * ratio)
        ratio = e_now * inverse
        ratio_buf[k] = ratio
        new_values = []
        for c in range(4):
            val = (d * (q[c] + 0.1 * growth[c]) + e_up * values[c]) * inverse
            val_buf[c, k] = val
            new_values.append(val)
        return acc_x, acc_y, force_u, force_v, e_now, ratio, tuple(new_values)

    zero = jnp.zeros((8, 128), F32)
    carry = (zero, zero, zero, zero, zero, zero, (zero, zero, zero, zero))

    def block_body(n, carry):
        g = n // per_group
        pl.when(n == per_group * g)(lambda: open_group(g))
        back = lax.rem(128 - 4 * BLOCK * (n - per_group * g), 128)
        rims = (
            [pltpu.roll(bq[c, g], back, 1) for c in range(4)],
            [pltpu.roll(bl[c, g], back, 1) for c in range(4)],
            [pltpu.roll(bcorn[c, g], back, 1) for c in range(2)],
        )
        pl.when(has_s)(lambda: to_north(n).wait_recv())
        pl.when(has_n)(lambda: to_south(n).wait_recv())
        for i in range(BLOCK):
            carry = level(n, i, rims, carry)
        return carry

    carry = lax.fori_loop(0, blocks, block_body, carry)

    for c in waits1:
        c.wait_recv()
    hand, handed = [], []
    for chip in range(chips):
        i = nxt()
        mate = dev(gx, tile_of(my_chip, 1 - core))
        have, want = tile_of(chip, core), tile_of(chip, 1 - core)
        hand.append(rc(all1.at[have], all1.at[have], i, mate))
        handed.append(rc(all1.at[want], all1.at[want], i, mate))
    scale = land_f / safe
    push1[0] = carry[2] * scale
    push1[1] = carry[3] * scale
    push_copies = pair(push1, p2recv)
    for c in push_copies:
        c.start()
    for c in hand:
        c.start()

    def back_body(n, state):
        after, mean_u, mean_v = state
        for i in range(BLOCK):
            k = levels - 1 - n * BLOCK - i
            ratio = ratio_buf[k]
            now = [val_buf[c, k] + ratio * after[c] for c in range(4)]
            val_buf[0, k] = now[0]
            val_buf[1, k] = now[1]
            val_buf[2, k] = now[2]
            val_buf[3, k] = now[3]
            part = jnp.where(k.astype(F32) < be, dz[k], 0.0)
            mean_u = mean_u + part * now[0]
            mean_v = mean_v + part * now[1]
            after = tuple(now)
        return after, mean_u, mean_v

    half = blocks // 3
    solved = lax.fori_loop(0, half, back_body, ((zero,) * 4, zero, zero))
    for c in push_copies:
        c.wait_recv()
    for f in range(2):
        wide2[2 * f] = push1[f]
        wide2[2 * f + 1] = jnp.where(lane < 64, p2recv[1, f], p2recv[0, f])
    starts2, waits2 = peers(wide2, all2)
    for c in starts2:
        c.start()
    all2[t] = wide2[...]
    unused, mean_u, mean_v = lax.fori_loop(half, blocks, back_body, solved)
    leaving = [
        pltpu.make_async_copy(val_buf.at[c], solved_out.at[c], load_sem.at[count_loads + c])
        for c in range(4)
    ]
    for c in leaving:
        c.start()

    count = 8 * tiles
    shape = (count, 128)
    lanes = lax.broadcasted_iota(jnp.int32, shape, 1)
    at_first, at_last = lanes == 0, lanes == 127
    for c in handed:
        c.wait_recv()
    body = pl.ds(8, count)
    above, below = pl.ds(9, count), pl.ds(7, count)
    for ref in (high, flow):
        for h in range(2):
            ref[h, 0:8, :] = jnp.zeros((8, 128), F32)
            ref[h, count + 8:count + 16, :] = jnp.zeros((8, 128), F32)
    for c in waits2:
        c.wait_recv()
    for tile in range(tiles):
        at = slice(8 * tile, 8 * tile + 8)
        f = all1[tile, 8]
        for h in range(2):
            depth = all1[tile, 6 + h]
            sea = jnp.where(depth > 0.0, 1.0, 0.0)
            state[0, h, at] = all1[tile, h]
            state[1, h, at] = all1[tile, 2 + h] * sea
            state[2, h, at] = all1[tile, 4 + h] * sea
            fixed[0, h, at] = sea
            fixed[5, h, at] = 1.25 * sea
            fixed[1, h, at] = 0.05 * depth
            fixed[2, h, at] = 0.1 * f * sea
            fixed[3, h, at] = 0.1 * all2[tile, h] * sea
            fixed[4, h, at] = 0.1 * all2[tile, 2 + h] * sea
    mine = rows_of(t)

    def diff_x(a):
        e = [pltpu.roll(x, 127, 1) for x in a]
        w = [pltpu.roll(x, 1, 1) for x in a]
        return [
            jnp.where(at_last, e[1 - h], e[h]) - jnp.where(at_first, w[1 - h], w[h])
            for h in range(2)
        ]

    def sub_body(i, sums):
        u = [state[1, h] for h in range(2)]
        v = [state[2, h] for h in range(2)]
        for h in range(2):
            flow[h, body] = fixed[1, h] * v[h]
        dx = diff_x([fixed[1, h] * u[h] for h in range(2)])
        tall = []
        for h in range(2):
            dy = flow[h, above] - flow[h, below]
            tall.append((state[0, h] - (dx[h] + dy)) * fixed[0, h])
            high[h, body] = tall[h]
            state[0, h] = tall[h]
        dx = diff_x(tall)
        for h in range(2):
            f, g = fixed[2, h], fixed[5, h]
            state[1, h] = u[h] + fixed[3, h] + f * v[h] - g * dx[h]
            state[2, h] = v[h] + fixed[4, h] - f * u[h] - g * (high[h, above] - high[h, below])
        return sums[0] + state[1, 0, mine], sums[1] + state[2, 0, mine]

    sum_u, sum_v = lax.fori_loop(0, NSUB, sub_body, (zero, zero))
    small_out[0] = state[0, 0, mine]
    small_out[1] = state[1, 0, mine]
    small_out[2] = state[2, 0, mine]
    small_out[3] = sum_u * (1.0 / NSUB) - mean_u / safe
    small_out[4] = sum_v * (1.0 / NSUB) - mean_v / safe
    small_out[5] = be

    for c in leaving:
        c.wait()
    for c in two_d + x_copies + starts1 + hand + push_copies + starts2:
        c.wait_send()
    norths = sum([diag_n(g) for g in range(groups)], []) + [be_up] + [to_north(n) for n in range(blocks)]
    souths = sum([diag_s(g) for g in range(groups)], []) + [be_down] + [to_south(n) for n in range(blocks)]
    for c in norths:
        pl.when(has_n)(c.wait_send)
    for c in souths:
        pl.when(has_s)(c.wait_send)


def settle(solved_in, small_in, vel_out, trc_out, surf_out, baro_out,
           solved, small, in_sem, out_sem):
    levels = solved_in.shape[1]
    half = levels // 2
    first = pltpu.make_async_copy(small_in, small, in_sem.at[0])
    first.start()
    trips = []
    for c in range(4):
        dst = vel_out if c < 2 else trc_out
        for at in (0, half):
            span = pl.ds(at, half)
            trips.append((c, at, solved_in.at[c, span], solved.at[c, span], dst.at[c % 2, span]))
    ins = [pltpu.make_async_copy(x[2], x[3], in_sem.at[1 + i]) for i, x in enumerate(trips)]
    outs = [pltpu.make_async_copy(x[3], x[4], out_sem.at[2 + i]) for i, x in enumerate(trips)]
    ends = [
        pltpu.make_async_copy(small.at[0], surf_out, out_sem.at[0]),
        pltpu.make_async_copy(small.at[pl.ds(1, 2)], baro_out, out_sem.at[1]),
    ]
    for c in ins:
        c.start()
    first.wait()
    for c in ends:
        c.start()
    be = small[5]
    for i, (c, at, *unused) in enumerate(trips):
        ins[i].wait()
        if c < 2:
            shift = small[3 + c]

            def body(n, carry):
                for j in range(BLOCK):
                    k = at + n * BLOCK + j
                    wet = k.astype(F32) < be
                    solved[c, k] = jnp.where(wet, solved[c, k] + shift, 0.0)
                return carry

            lax.fori_loop(0, half // BLOCK, body, 0)
        outs[i].start()
    for c in ends + outs:
        c.wait()


def shards(nx, ngy, nga, velocity, tracers, mixing, thickness, coriolis, land, bottom, surface, barotropic):
    levels = thickness.shape[0]
    tiles = ngy * nga
    groups = (levels + 31) // 32
    copies = 4 + 2 * (levels // BLOCK) + 2 + 4 * groups + (tiles - 1) + 2 + (tiles - 1)
    tile = (8, 128)
    scratch = [
        (levels,) + tile, (levels,) + tile, (levels,) + tile, (levels,) + tile,
        (6, groups) + tile, (2, 4, groups) + tile, (2, groups) + tile, (2, groups) + tile,
        (4, groups) + tile, (4, groups) + tile, (2, groups) + tile,
        (5,) + tile, (2, 5) + tile, (9,) + tile, (tiles, 9) + tile,
        (2,) + tile, (2, 2) + tile, (4,) + tile, (tiles, 4) + tile,
        (levels,) + tile, (4, levels) + tile, tile, tile,
        (3, 2, 8 * tiles, 128), (6, 2, 8 * tiles, 128), (2, 8 * tiles + 16, 128), (2, 8 * tiles + 16, 128),
    ]
    staged = [
        pltpu.VMEM(velocity.shape, F32), pltpu.VMEM(tracers.shape, F32), pltpu.VMEM(mixing.shape, F32),
        pltpu.SMEM(thickness.shape, F32), pltpu.SMEM(coriolis.shape, F32),
        pltpu.VMEM(land.shape, jnp.int32), pltpu.VMEM(bottom.shape, jnp.int32),
        pltpu.VMEM(surface.shape, F32), pltpu.VMEM(barotropic.shape, F32),
    ]
    vmem = pl.BlockSpec(memory_space=pltpu.VMEM)
    far = pl.BlockSpec(memory_space=pltpu.HBM)
    results = pl.pallas_call(
        functools.partial(kernel, nx, ngy, nga, levels),
        out_shape=(
            jax.ShapeDtypeStruct((4, levels) + tile, F32),
            jax.ShapeDtypeStruct((6,) + tile, F32),
        ),
        in_specs=[far] * 9,
        out_specs=(far, vmem),
        scratch_shapes=[pltpu.VMEM(s, F32) for s in scratch]
        + staged
        + [pltpu.SemaphoreType.DMA((copies,)), pltpu.SemaphoreType.DMA((copies,)), pltpu.SemaphoreType.DMA((19,))],
        compiler_params=pltpu.CompilerParams(
            collective_id=0, has_side_effects=True, vmem_limit_bytes=64 * 1024 * 1024
        ),
    )(velocity, tracers, mixing, thickness, coriolis, land, bottom, surface, barotropic)
    anywhere = pl.BlockSpec(memory_space=pltpu.HBM)
    return pl.pallas_call(
        settle,
        out_shape=tuple(
            jax.ShapeDtypeStruct(r.shape, F32) for r in (velocity, tracers, surface, barotropic)
        ),
        in_specs=[anywhere] * 2,
        out_specs=(anywhere,) * 4,
        scratch_shapes=[pltpu.VMEM(r.shape, F32) for r in results]
        + [pltpu.SemaphoreType.DMA((10,)), pltpu.SemaphoreType.DMA((10,))],
        compiler_params=pltpu.CompilerParams(vmem_limit_bytes=64 * 1024 * 1024),
    )(*results)


def solution(mesh):
    sizes = mesh.shape
    return jax.shard_map(
        functools.partial(shards, sizes["gx"], sizes["gy"], sizes["ga"]),
        mesh=mesh,
        in_specs=(
            P(None, None, ("gy", "ga"), "gx"),
            P(None, None, ("gy", "ga"), "gx"),
            P(None, ("gy", "ga"), "gx"),
            P(),
            P(("gy", "ga")),
            P(("gy", "ga"), "gx"),
            P(("gy", "ga"), "gx"),
            P(("gy", "ga"), "gx"),
            P(None, ("gy", "ga"), "gx"),
        ),
        out_specs=(
            P(None, None, ("gy", "ga"), "gx"),
            P(None, None, ("gy", "ga"), "gx"),
            P(("gy", "ga"), "gx"),
            P(None, ("gy", "ga"), "gx"),
        ),
        check_vma=False,
    )
```
